128 devices in a mesh: gx: 8 (over x, core), gy: 16 (over z, y).
Axes of the slice: x: 4, y: 4, z: 4, core: 2. Of those that a mesh axis runs over, the one named last changes fastest.
Arguments:
- traction: bfloat16 [3, 289, 8, 16, 512], P(None, None, 'gx', 'gy'), may hold values from -6 to 6
- self_operator: bfloat16 [289, 289], replicated, may hold values from -0.375 to 0.375
- translation: bfloat16 [289, 289], replicated, may hold values from -0.09375 to 0.09375
- rotations: bfloat16 [16, 289, 289], replicated
- own_cell: int32 [8, 16, 9, 128], P('gx', 'gy'), may hold values from 0 to 511
- partner_cell: int32 [8, 16, 9, 128], P('gx', 'gy'), may hold values from 0 to 511
- rot_index: int32 [8, 16, 9, 128, 1], P('gx', 'gy'), may hold values from 0 to 15; in each aligned block of 128 rows (0 to 127, 128 to 255, ..., all dimensions but the last counted through in order) at most 16 rows name the same one
- block_count: int32 [8, 16, 9], P('gx', 'gy'), may hold values from 1 to 128, as said below
Outputs:
- velocity: bfloat16 [3, 289, 8, 16, 512], P(None, None, 'gx', 'gy')
The draws below stay inside these ranges and needn't reach their ends.
Inputs may be any that keep to these rules, and one draw needn't show every extreme that they name: `rot_index`: in each owner pair block of 128 slots no rotation index is named by more than 16 slots, and in every draw some block reaches 16. `block_count`: some block of some region is full in every draw; regions differ in density.
All inputs are finite; a program needn't handle non-finite values.
Results may differ from the reference program's by a relative error of at most 0.0036.
Values may be sent and summed in bfloat16 or wider, within the bound.
No kernel may reach another device: no remote copies, remote signals or barrier semaphores. Data moves between devices by JAX's collectives and lax.ppermute only.
A program may use at most 128 MiB of HBM per device.

```python
import math
import jax
import jax.numpy as jnp
import numpy as np
from jax import lax

K = 289
NR = 16
CELL_DEV = 512
BLOCK = 128
MOST = 16
CAP = 144
N_GX = 8
N_GY = 16


def degree_mask(size_k):
    positions = jnp.arange(size_k, dtype=jnp.int32)
    squares = positions * positions
    degree = jnp.sum((positions[:, None] >= squares[None, :]).astype(jnp.int32), axis=1).astype(jnp.int32) - 1
    same = (degree[:, None] == degree[None, :]).astype(jnp.float32)
    widths = jnp.sqrt((2 * degree + 1).astype(jnp.float32))
    return same / widths[:, None]


def draw_rotations(key, part):
    key = jax.random.fold_in(key, 11)
    noise = jax.random.normal(key, (NR, K, K), jnp.float32) * 0.5
    eye_table = jnp.eye(K, dtype=jnp.float32)[None, :, :]
    return (eye_table + noise * degree_mask(K)[None, :, :]).astype(jnp.bfloat16)


def draw_block_count(key, part):
    key = jax.random.fold_in(key, 7)
    first, second, third = jax.random.split(key, 3)
    base = jax.random.randint(first, (N_GX, N_GY, 9), 1, BLOCK // 2 + 1, dtype=jnp.int32)
    dense = jax.random.randint(second, (N_GX, N_GY, 1), 1, 5, dtype=jnp.int32)
    counts = jnp.minimum(base * dense, BLOCK)
    chosen = jax.random.randint(third, (), 0, N_GX * N_GY * 9, dtype=jnp.int32)
    flat_pos = jnp.arange(N_GX * N_GY * 9, dtype=jnp.int32).reshape(N_GX, N_GY, 9)
    return jnp.where(flat_pos == chosen, BLOCK, counts).astype(jnp.int32)


def with_ends(array, key, smallest, top_value):
    longest = array.shape.index(max(array.shape))
    spots = []
    for shift in (0, 1):
        where = [jax.random.randint(jax.random.fold_in(key, axis), (), 0, length) for axis, length in enumerate(array.shape)]
        where[longest] = (where[longest] + shift) % array.shape[longest]
        spots.append(tuple(where))
    return array.at[spots[0]].set(smallest).at[spots[1]].set(top_value)


def level_of(rng, extent, pieces, smallest, largest):
    loudness = 1.0
    for dim, shards_of in pieces:
        steps = jax.random.uniform(jax.random.fold_in(jax.random.fold_in(rng, 6), dim), (shards_of,), jnp.float32, smallest / len(pieces), largest / len(pieces))
        loudness = loudness * jnp.repeat(jnp.exp(steps), extent[dim] // shards_of).reshape((-1,) + (1,) * (len(extent) - 1 - dim))
    return loudness


def shared_out(stream_key, own, number, rows, amount, top, most, skew):
    order = jax.random.permutation(stream_key, amount)
    crowded, usual = portions_of(amount, rows * top, most, skew, True), portions_of(amount, rows * top, most, skew, False)
    places = jnp.arange(amount)

    def named(lengths, rotation):
        used = int((lengths > 0).sum())
        fixed = max(1, used // 4)
        moved = fixed + (places - fixed + rotation * (used - fixed)) % max(1, amount - fixed)
        return jnp.zeros((amount,), jnp.int32).at[order[jnp.where(places < fixed, places, moved)]].set(jnp.asarray(lengths, jnp.int32))

    lengths = jnp.where(number % 4 == 0, named(crowded, number // 4), named(usual, number - number // 4 - 1))
    mixed = jax.random.permutation(jax.random.fold_in(own, 3), amount)
    giver, sink = mixed[0:amount // 2 * 2:2], mixed[1:amount // 2 * 2:2]
    margin = jnp.minimum(lengths[giver] - 1, most - lengths[sink]) // 2
    margin = jnp.where((giver == order[0]) | (sink == order[0]) | (lengths[sink] == 0), 0, jnp.maximum(margin, 0))
    moved = jax.random.randint(jax.random.fold_in(own, 4), (amount // 2,), 0, 1 << 20) % (margin + 1)
    lengths = lengths.at[giver].add(-moved).at[sink].add(moved)
    items = jnp.searchsorted(jnp.cumsum(lengths), jnp.arange(rows * top), side="right").astype(jnp.int32)
    grid = items.reshape(top, rows).T
    grid = grid[jax.random.permutation(jax.random.fold_in(own, 1), rows)]
    rotation = jax.random.randint(jax.random.fold_in(own, 2), (rows, 1), 0, top)
    return jnp.take_along_axis(grid, (jnp.arange(top)[None, :] + rotation) % top, axis=1)


def portions_of(number_of, total, reach, slope, full):
    weights = [(1 << 20) // math.isqrt(grade ** slope) + 1 for grade in range(1, number_of + 1)]
    largest = reach if full else min(reach, max(-(-total // number_of), total * weights[0] // sum(weights)))
    least = 1 if total - largest >= number_of - 1 else 0
    given, spare = [largest] + [least] * (number_of - 1), total - largest - least * (number_of - 1)
    while spare > 0:
        movable = [i for i in range(1, number_of) if given[i] < largest] or [i for i in range(1, number_of) if given[i] < reach]
        pool, remaining = sum([weights[i] for i in movable]), spare
        for i in movable:
            addition = min(reach - given[i], max(1, remaining * weights[i] // pool), spare)
            given[i] = given[i] + addition
            spare = spare - addition
    return np.array(given)


def centred(own_key, shape, scale, most, pieces=(), held_as=jnp.bfloat16):
    gain = level_of(own_key, shape, pieces, -0.22, 0.18) if pieces else 1.0
    array = jax.random.normal(own_key, shape, jnp.float32) * scale * gain
    return jnp.minimum(jnp.maximum(array, -most), most).astype(held_as)


def setup_inputs(seed: int = 0) -> dict:
    splits = jax.random.split(jax.random.key(seed), 9)
    traction = centred(splits[0], (3, K, N_GX, N_GY, CELL_DEV), 1.0, 6.0, ((2, 8), (3, 16)))
    self_operator = centred(splits[1], (K, K), K ** -0.5, 0.375)
    translation = centred(splits[2], (K, K), (16 * K) ** -0.5, 0.09375)
    rotations = draw_rotations(jax.random.fold_in(splits[8], 71), 0)
    own_cell = with_ends(jax.random.randint(splits[4], (N_GX, N_GY, 9, BLOCK), 0, CELL_DEV), jax.random.fold_in(splits[4], 1), 0, CELL_DEV - 1).astype(jnp.int32)
    partner_cell = with_ends(jax.random.randint(splits[5], (N_GX, N_GY, 9, BLOCK), 0, CELL_DEV), jax.random.fold_in(splits[5], 1), 0, CELL_DEV - 1).astype(jnp.int32)
    rot_index_keys = jax.random.split(jax.random.fold_in(splits[6], 1), N_GX * N_GY * 9 * BLOCK // BLOCK)
    rot_index_turns = jax.random.permutation(jax.random.fold_in(splits[6], 3), N_GX * N_GY * 9 * BLOCK // BLOCK)
    rot_index = jax.vmap(lambda own, number: shared_out(jax.random.fold_in(splits[6], 2), own, number, BLOCK, NR, 1, MOST, 1))(rot_index_keys, rot_index_turns).reshape((N_GX, N_GY, 9, BLOCK, 1))
    block_count = draw_block_count(jax.random.fold_in(splits[8], 71), 0)
    return {"traction": traction, "self_operator": self_operator, "translation": translation, "rotations": rotations, "own_cell": own_cell, "partner_cell": partner_cell, "rot_index": rot_index, "block_count": block_count}


def parity_signs(size_k):
    positions = jnp.arange(size_k, dtype=jnp.int32)
    squares = positions * positions
    degree = jnp.sum((positions[:, None] >= squares[None, :]).astype(jnp.int32), axis=1).astype(jnp.int32) - 1
    return (1 - 2 * (degree % 2)).astype(jnp.float32)


def group_slots(rot_flat, live_flat, rot_count, capacity):
    slot_total = rot_flat.shape[0]
    onehot = (rot_flat[:, None] == jnp.arange(rot_count, dtype=jnp.int32)[None, :]).astype(jnp.int32)
    before = (jnp.cumsum(onehot, axis=0).astype(jnp.int32) - onehot).astype(jnp.int32)
    position = jnp.sum(before * onehot, axis=1).astype(jnp.int32)
    target = (rot_flat * capacity + position).astype(jnp.int32)
    slot_table = jnp.zeros((rot_count * capacity,), jnp.int32).at[target].set(jnp.arange(slot_total, dtype=jnp.int32))
    weights = jnp.zeros((rot_count * capacity,), jnp.float32).at[target].set(live_flat)
    return slot_table, weights


def round_keep(values):
    return lax.optimization_barrier(values.astype(jnp.bfloat16)).astype(jnp.float32)


def pair_terms(own_group, partner_group, rot32, trans32, parity, weights):
    own_turned = round_keep(jnp.einsum("rkl,clrn->rckn", rot32, own_group))
    partner_turned = round_keep(jnp.einsum("rkl,clrn->rckn", rot32, partner_group))
    toward_own = round_keep(jnp.einsum("kl,rcln->rckn", trans32, partner_turned))
    sign_flip = parity[None, None, :, None]
    toward_partner = round_keep(jnp.einsum("kl,rcln->rckn", trans32, own_turned * sign_flip) * sign_flip)
    back_own = jnp.einsum("rlk,rcln->ckrn", rot32, toward_own) * weights[None, None]
    back_partner = jnp.einsum("rlk,rcln->ckrn", rot32, toward_partner) * weights[None, None]
    out_shape = (back_own.shape[0], back_own.shape[1], -1)
    return back_own.reshape(out_shape), back_partner.reshape(out_shape)


def reference(traction, self_operator, translation, rotations, own_cell, partner_cell, rot_index, block_count):
    size_k = traction.shape[1]
    grid_x = traction.shape[2]
    grid_y = traction.shape[3]
    cell_count = traction.shape[4]
    slot_count = own_cell.shape[3]
    rot_count = rotations.shape[0]
    capacity = CAP
    regions = grid_x * grid_y
    parity = parity_signs(size_k)
    rot32 = rotations.astype(jnp.float32)
    trans32 = translation.astype(jnp.float32)
    shifted = jnp.stack([jnp.roll(traction, (1 - offset // 3, 1 - offset % 3), axis=(2, 3)) for offset in range(9)], axis=2)
    neighbours = jnp.transpose(shifted, (3, 4, 0, 1, 2, 5)).reshape(regions, 3, size_k, 9 * cell_count)
    own_coef = jnp.transpose(traction, (2, 3, 0, 1, 4)).reshape(regions, 3, size_k, cell_count)
    device_items = (own_coef, neighbours, own_cell.reshape(regions, 9, slot_count),
                    partner_cell.reshape(regions, 9, slot_count), rot_index.reshape(regions, 9 * slot_count),
                    block_count.reshape(regions, 9))

    def one_device(items_here):
        own_here, near_coefs, own_slots, partner_slots, rot_flat, counts = items_here
        live_flat = (jnp.arange(slot_count, dtype=jnp.int32)[None, :] < counts[:, None]).astype(jnp.float32).reshape(-1)
        own_flat = own_slots.reshape(-1)
        partner_flat = (partner_slots + (jnp.arange(9, dtype=jnp.int32) * cell_count)[:, None]).reshape(-1)
        slot_table, weights = group_slots(rot_flat, live_flat, rot_count, capacity)
        own_index = own_flat[slot_table]
        partner_index = partner_flat[slot_table]
        own_group = jnp.take(own_here, own_index, axis=2).reshape(3, size_k, rot_count, capacity).astype(jnp.float32)
        partner_group = jnp.take(near_coefs, partner_index, axis=2).reshape(3, size_k, rot_count, capacity).astype(jnp.float32)
        back_own, back_partner = pair_terms(own_group, partner_group, rot32, trans32, parity,
                                            weights.reshape(rot_count, capacity))
        own_sum = jnp.zeros((3, size_k, cell_count), jnp.float32).at[:, :, own_index].add(back_own)
        outgoing = jnp.zeros((3, size_k, 9 * cell_count), jnp.float32).at[:, :, partner_index].add(back_partner)
        return own_sum, outgoing

    own_sums, outgoing = lax.map(one_device, device_items)
    outgoing = outgoing.reshape(grid_x, grid_y, 3, size_k, 9, cell_count)
    received = jnp.zeros((grid_x, grid_y, 3, size_k, cell_count), jnp.float32)
    for offset in range(9):
        received = received + jnp.roll(outgoing[:, :, :, :, offset], (offset // 3 - 1, offset % 3 - 1), axis=(0, 1))
    self_term = jnp.einsum("kl,gcln->gckn", self_operator.astype(jnp.float32), own_coef.astype(jnp.float32))
    summed = self_term + own_sums + received.reshape(regions, 3, size_k, cell_count)
    velocity = summed.astype(jnp.bfloat16).reshape(grid_x, grid_y, 3, size_k, cell_count)
    return jnp.transpose(velocity, (2, 3, 0, 1, 4))
```

```python
import functools

import jax
import jax.numpy as jnp
from jax import lax
from jax.experimental import pallas as pl
from jax.experimental.pallas import tpu as pltpu
from jax.sharding import PartitionSpec as P

BF = jnp.bfloat16
F32 = jnp.float32

K = 289
MAIN = 256
REST = K - MAIN
TAIL = 128
WIDE = 3 * MAIN + TAIL
CELLS = 512
SLOTS = 128
NR = 16
CAP = 16
PAIR = 2 * SLOTS
GROUP = 2 * CAP
ROWS = NR * GROUP
OWN, PARTNER, ROT, META = 0, 9, 18, 32
VMEM_LIMIT = 48 * 1024 * 1024


def nt(a, b):
    return lax.dot_general(a, b, (((1,), (1,)), ((), ())), preferred_element_type=F32)


def nn(a, b):
    return jnp.dot(a, b, preferred_element_type=F32)


def iota(shape, dim):
    return lax.broadcasted_iota(jnp.int32, shape, dim)


def where_one(condition):
    return jnp.where(condition, 1.0, 0.0).astype(BF)


def eye(size):
    return where_one(iota((size, size), 0) == iota((size, size), 1))


def spread(c):
    return where_one(iota((TAIL, REST), 0) == iota((TAIL, REST), 1) + c * REST)


def offset_of(dx, dy):
    return (dx + 1) * 3 + dy + 1


def parity_lanes(width, start):
    k = iota((1, width), 1) + start
    degree = jnp.zeros((1, width), jnp.int32)
    for level in range(1, 17):
        degree = degree + jnp.where(k >= level * level, 1, 0)
    return 1.0 - 2.0 * (degree % 2).astype(F32)


def side_signs(width, start):
    signs = jnp.broadcast_to(parity_lanes(width, start), (GROUP, width))
    return jnp.where(iota((GROUP, width), 0) >= CAP, signs, 1.0)


def pick_table(own_side, partner_side):
    cells = iota((CELLS, SLOTS), 0)
    return jnp.concatenate([where_one(cells == own_side), where_one(cells == partner_side)], axis=1)


def tail_of(parts):
    total = None
    for c, part in enumerate(parts):
        term = nn(spread(c), part)
        total = term if total is None else total + term
    return total.astype(BF)


def positions(rots):
    marks = [where_one(iota((NR, SLOTS), 0) == rot) for rot in rots]
    earlier = where_one(iota((SLOTS, SLOTS), 0) < iota((SLOTS, SLOTS), 1))
    ranks = nn(jnp.concatenate(marks, axis=0), earlier)
    places = []
    for j, mark in enumerate(marks):
        base = (iota((NR, SLOTS), 0) * GROUP + (j % 2) * CAP + 1).astype(F32)
        values = mark.astype(F32) * (ranks[j * NR : (j + 1) * NR] + base)
        places.append(jnp.sum(values, axis=0, keepdims=True).astype(jnp.int32) - 1)
    return places


def apply_dense(mains, tail, main_ref, to_tail_ref, from_tail_ref, tail_ref):
    size = mains[0].shape[0]
    middle = nt(jnp.concatenate(mains, axis=0), main_ref[:MAIN, :MAIN])
    out_tail = nt(tail, tail_ref[...])
    outs = []
    for c in range(3):
        outs.append(middle[c * size : (c + 1) * size] + nt(tail, from_tail_ref[c]))
        out_tail = out_tail + nt(mains[c], to_tail_ref[c])
    return outs, out_tail


def split_lanes(block):
    return [block[:, c * MAIN : (c + 1) * MAIN] for c in range(3)], block[:, 3 * MAIN :]


def prep_kernel(rot_ref, trans_ref, self_ref, rot_tail, *pieces):
    fold = where_one((iota((TAIL, REST), 0) % REST == iota((TAIL, REST), 1)) & (iota((TAIL, REST), 0) < 3 * REST))
    same = (iota((TAIL, TAIL), 0) // REST) == (iota((TAIL, TAIL), 1) // REST)

    def tail_block(block):
        return jnp.where(same, nt(nn(fold, block).astype(BF), fold), 0.0).astype(BF)

    for r in range(NR):
        rot_tail[r] = tail_block(rot_ref[r, MAIN:, MAIN:])
    for source, (to_tail, from_tail, tail) in ((trans_ref, pieces[:3]), (self_ref, pieces[3:])):
        for c in range(3):
            to_tail[c] = nn(spread(c), source[MAIN:, :MAIN]).astype(BF)
            from_tail[c] = nt(source[:MAIN, MAIN:], spread(c)).astype(BF)
        tail[...] = tail_block(source[MAIN:, MAIN:])


def pick_kernel(rows, count, *refs):
    sources, meta, left, right = refs[:count], refs[count], refs[count + 1], refs[count + 2]
    to_left, to_right = refs[count + 3 :]
    for i, (source, dy) in enumerate(zip(sources, rows)):
        for ex, target, out in ((-1, left, to_left), (1, right, to_right)):
            o = offset_of(-ex, dy)
            table = pick_table(
                target[1, PARTNER + o : PARTNER + o + 1, :], meta[dy + 1, OWN + 8 - o : OWN + 9 - o, :]
            )
            for c in range(3):
                out[i, c] = nn(source[c], table).astype(BF)


def phase_kernel(sources, whole, first, last, *refs):
    m = len(sources)
    arrays = refs[: (m if last is False else 2)]
    refs = refs[len(arrays) :]
    meta, left, right, rot_ref, rot_tail, trans_ref, t1, t2, t3 = refs[:9]
    refs = refs[9:]
    if first:
        self_ref, s1, s2, s3 = refs[:4]
        refs = refs[4:]
    else:
        acc_in = refs[0]
        refs = refs[1:]
    out, picked, grouped, turned, places_to = refs[:5]
    acc = refs[5] if last else out

    def meta_row(dx, dy, row):
        return (left, meta, right)[dx + 1][dy + 1, row : row + 1, :]

    def slot_rows(dx, dy, mine, theirs):
        o = offset_of(dx, dy)
        return meta_row(0, 0, mine + o), meta_row(dx, dy, theirs + 8 - o)

    if first:
        unit = eye(CELLS)
        here = arrays[0]
        mains = [nt(unit, here[c, :MAIN, :]).astype(BF) for c in range(3)]
        tail = nt(unit, tail_of([here[c, MAIN:, :] for c in range(3)])).astype(BF)
        outs, out_tail = apply_dense(mains, tail, self_ref, s1, s2, s3)
        for c in range(3):
            acc[:, c * MAIN : (c + 1) * MAIN] = outs[c]
        acc[:, 3 * MAIN :] = out_tail

    rots = []
    for dx, dy in sources:
        rots.extend(slot_rows(dx, dy, ROT, ROT))
    places = positions(rots)

    for s, (dx, dy) in enumerate(sources):
        if s < whole:
            table = pick_table(*slot_rows(dx, dy, PARTNER, OWN))
            for c in range(3):
                picked[c] = nn(arrays[s][c], table).astype(BF)
            taken = [picked[c] for c in range(3)]
        elif last:
            side, which = arrays[0 if dx < 0 else 1], (0 if dy < 0 else 1)
            taken = [side[which, c] for c in range(3)]
        else:
            taken = [arrays[s][0, c] for c in range(3)]
        row_ids = iota((ROWS, SLOTS), 0)
        own_place, partner_place = places[2 * s], places[2 * s + 1]
        place = jnp.concatenate([where_one(row_ids == own_place), where_one(row_ids == partner_place)], axis=1)
        lanes = slice(s * GROUP, (s + 1) * GROUP)
        for c in range(3):
            grouped[:, lanes, c * MAIN : (c + 1) * MAIN] = (
                nt(place, taken[c][:MAIN]).astype(BF).reshape(NR, GROUP, MAIN)
            )
        grouped[:, lanes, 3 * MAIN :] = (
            nt(place, tail_of([t[MAIN:] for t in taken])).astype(BF).reshape(NR, GROUP, TAIL)
        )
        own_to, partner_to = slot_rows(dx, dy, OWN, PARTNER)
        to = jnp.concatenate([own_to, partner_to], axis=1) + 1
        digits = jnp.concatenate([to // 32, to % 32, jnp.zeros((6, PAIR), jnp.int32)], axis=0)
        back = nt(digits.astype(F32).astype(BF), place)
        goal = (back[0:1] * 32.0 + back[1:2]).astype(jnp.int32) - 1
        places_to[:, s * ROWS : (s + 1) * ROWS] = where_one(iota((CELLS, ROWS), 0) == goal)

    size = m * GROUP
    main_signs = side_signs(MAIN, 0)
    tail_signs = side_signs(TAIL, MAIN)

    def turn(r, source, target, dot):
        block = source[r]
        mains, tail = split_lanes(block)
        turned_main = dot(jnp.concatenate(mains, axis=0), rot_ref[r, :MAIN, :MAIN])
        turned_main = (turned_main.reshape(3 * m, GROUP, MAIN) * main_signs[None]).reshape(3 * size, MAIN)
        for c in range(3):
            target[r, :, c * MAIN : (c + 1) * MAIN] = turned_main[c * size : (c + 1) * size].astype(BF)
        target[r, :, 3 * MAIN :] = dot(tail, rot_tail[r]).astype(BF)

    for r in range(NR):
        turn(r, grouped, turned, nt)

    step = 4

    def translate(i, carry):
        block = turned[pl.ds(i * step, step)].reshape(step * size, WIDE)
        mains, tail = split_lanes(block)
        outs, out_tail = apply_dense(mains, tail, trans_ref, t1, t2, t3)
        for c in range(3):
            grouped[pl.ds(i * step, step), :, c * MAIN : (c + 1) * MAIN] = (
                outs[c].astype(BF).reshape(step, size, MAIN)
            )
        grouped[pl.ds(i * step, step), :, 3 * MAIN :] = out_tail.astype(BF).reshape(step, size, TAIL)
        return carry

    lax.fori_loop(0, NR // step, translate, 0)

    for r in range(NR):
        turn(r, grouped, turned, nn)

    columns = [slice(c * MAIN, (c + 1) * MAIN) for c in range(3)] + [slice(3 * MAIN, WIDE)]
    for lanes in columns:
        total = acc[:, lanes] if first else acc_in[:, lanes]
        for s in range(m):
            back = turned[:, s * GROUP : (s + 1) * GROUP, lanes].reshape(ROWS, lanes.stop - lanes.start)
            total = total + nn(places_to[:, s * ROWS : (s + 1) * ROWS], back)
        acc[:, lanes] = total

    if last:
        unit = eye(MAIN)
        tail = acc[:, 3 * MAIN :].astype(BF)
        for c in range(3):
            out[c, :MAIN, :] = nt(unit, acc[:, c * MAIN : (c + 1) * MAIN].astype(BF)).astype(BF)
            gather = where_one(iota((REST, TAIL), 1) == iota((REST, TAIL), 0) + c * REST)
            out[c, MAIN:, :] = nt(gather, tail).astype(BF)


def vmem_call(kernel, out_shape, scratch=(), flops=0):
    return pl.pallas_call(
        kernel,
        out_shape=out_shape,
        scratch_shapes=list(scratch),
        compiler_params=pltpu.CompilerParams(vmem_limit_bytes=VMEM_LIMIT),
        cost_estimate=pl.CostEstimate(flops=flops, bytes_accessed=8_000_000, transcendentals=0),
    )


def phase_call(sources, whole, first, last):
    m = len(sources)
    if last:
        out = jax.ShapeDtypeStruct((3, K, CELLS), BF)
    else:
        out = jax.ShapeDtypeStruct((CELLS, WIDE), F32)
    scratch = [
        pltpu.VMEM((3, K, PAIR), BF),
        pltpu.VMEM((NR, m * GROUP, WIDE), BF),
        pltpu.VMEM((NR, m * GROUP, WIDE), BF),
        pltpu.VMEM((CELLS, m * ROWS), BF),
    ]
    if last:
        scratch.append(pltpu.VMEM((CELLS, WIDE), F32))
    kernel = functools.partial(phase_kernel, sources, whole, first, last)
    return vmem_call(kernel, out, scratch, flops=m * 4_000_000_000)


def shift(block, axis, distance):
    count = lax.axis_size(axis)
    return lax.ppermute(block, axis, [((i - distance) % count, i) for i in range(count)])


def local(traction, self_operator, translation, rotations, own_cell, partner_cell, rot_index, block_count):
    here = traction.reshape(3, K, CELLS)
    live = iota((9, SLOTS), 1) < block_count.reshape(9, 1)
    rot = jnp.where(live, rot_index.reshape(9, SLOTS), NR)
    meta = jnp.concatenate(
        [own_cell.reshape(9, SLOTS), partner_cell.reshape(9, SLOTS), rot, jnp.zeros((META - 27, SLOTS), jnp.int32)]
    )
    meta_low, meta_high = shift(meta, "gy", 1), shift(meta, "gy", -1)
    low, high = shift(here, "gy", 1), shift(here, "gy", -1)
    meta = jnp.stack([meta_low, meta, meta_high])
    left, right = shift(meta, "gx", 1), shift(meta, "gx", -1)
    metas = (meta, left, right)

    picked = jax.ShapeDtypeStruct((1, 3, K, PAIR), BF)
    to_left, to_right = vmem_call(
        functools.partial(pick_kernel, (0,), 1), (picked, picked), flops=1_000_000_000
    )(here, *metas)
    from_left, from_right = shift(to_right, "gx", 1), shift(to_left, "gx", -1)

    dense = [
        jax.ShapeDtypeStruct((3, TAIL, MAIN), BF),
        jax.ShapeDtypeStruct((3, MAIN, TAIL), BF),
        jax.ShapeDtypeStruct((TAIL, TAIL), BF),
    ]
    rot_tail, t1, t2, t3, s1, s2, s3 = vmem_call(
        prep_kernel, [jax.ShapeDtypeStruct((NR, TAIL, TAIL), BF)] + dense + dense, flops=100_000_000
    )(rotations, translation, self_operator)
    weights = (rotations, rot_tail, translation, t1, t2, t3)

    acc = phase_call(((0, 0), (-1, 0), (1, 0)), 1, True, False)(
        here, from_left, from_right, *metas, *weights, self_operator, s1, s2, s3
    )

    picked = jax.ShapeDtypeStruct((2, 3, K, PAIR), BF)
    to_left, to_right = vmem_call(
        functools.partial(pick_kernel, (-1, 1), 2), (picked, picked), flops=2_000_000_000
    )(low, high, *metas)
    from_left, from_right = shift(to_right, "gx", 1), shift(to_left, "gx", -1)

    acc = phase_call(((0, -1), (0, 1)), 2, False, False)(low, high, *metas, *weights, acc)
    velocity = phase_call(((-1, -1), (-1, 1), (1, -1), (1, 1)), 0, False, True)(
        from_left, from_right, *metas, *weights, acc
    )
    return velocity.reshape(3, K, 1, 1, CELLS)


def solution(mesh):
    return jax.shard_map(
        local,
        mesh=mesh,
        in_specs=(
            P(None, None, "gx", "gy", None),
            P(),
            P(),
            P(),
            P("gx", "gy", None, None),
            P("gx", "gy", None, None),
            P("gx", "gy", None, None, None),
            P("gx", "gy", None),
        ),
        out_specs=P(None, None, "gx", "gy", None),
        check_vma=False,
    )
```

```python
import functools

import jax
import jax.numpy as jnp
from jax import lax
from jax.experimental import pallas as pl
from jax.experimental.pallas import tpu as pltpu
from jax.sharding import PartitionSpec as P

BF = jnp.bfloat16
F32 = jnp.float32

K = 289
MAIN = 256
REST = K - MAIN
TAIL = 128
WIDE = 3 * MAIN + TAIL
CELLS = 512
SLOTS = 128
NR = 16
CAP = 16
PAIR = 2 * SLOTS
GROUP = 2 * CAP
ROWS = NR * GROUP
OWN, PARTNER, ROT, META = 0, 9, 18, 32
VMEM_LIMIT = 48 * 1024 * 1024


def nt(a, b):
    return lax.dot_general(a, b, (((1,), (1,)), ((), ())), preferred_element_type=F32)


def nn(a, b):
    return jnp.dot(a, b, preferred_element_type=F32)


def iota(shape, dim):
    return lax.broadcasted_iota(jnp.int32, shape, dim)


def where_one(condition):
    return jnp.where(condition, 1.0, 0.0).astype(BF)


def eye(size):
    return where_one(iota((size, size), 0) == iota((size, size), 1))


def spread(c):
    return where_one(iota((TAIL, REST), 0) == iota((TAIL, REST), 1) + c * REST)


def offset_of(dx, dy):
    return (dx + 1) * 3 + dy + 1


def parity_lanes(width, start):
    k = iota((1, width), 1) + start
    degree = jnp.zeros((1, width), jnp.int32)
    for level in range(1, 17):
        degree = degree + jnp.where(k >= level * level, 1, 0)
    return 1.0 - 2.0 * (degree % 2).astype(F32)


def side_signs(width, start):
    signs = jnp.broadcast_to(parity_lanes(width, start), (GROUP, width))
    return jnp.where(iota((GROUP, width), 0) >= CAP, signs, 1.0)


def pick_table(own_side, partner_side):
    cells = iota((CELLS, SLOTS), 0)
    return jnp.concatenate([where_one(cells == own_side), where_one(cells == partner_side)], axis=1)


def tail_of(parts):
    total = None
    for c, part in enumerate(parts):
        term = nn(spread(c), part)
        total = term if total is None else total + term
    return total.astype(BF)


def positions(rots):
    marks = [where_one(iota((NR, SLOTS), 0) == rot) for rot in rots]
    earlier = where_one(iota((SLOTS, SLOTS), 0) < iota((SLOTS, SLOTS), 1))
    ranks = nn(jnp.concatenate(marks, axis=0), earlier)
    places = []
    for j, mark in enumerate(marks):
        base = (iota((NR, SLOTS), 0) * GROUP + (j % 2) * CAP + 1).astype(F32)
        values = mark.astype(F32) * (ranks[j * NR : (j + 1) * NR] + base)
        places.append(jnp.sum(values, axis=0, keepdims=True).astype(jnp.int32) - 1)
    return places


def apply_dense(mains, tail, main_ref, to_tail_ref, from_tail_ref, tail_ref):
    size = mains[0].shape[0]
    middle = nt(jnp.concatenate(mains, axis=0), main_ref[:MAIN, :MAIN])
    out_tail = nt(tail, tail_ref[...])
    outs = []
    for c in range(3):
        outs.append(middle[c * size : (c + 1) * size] + nt(tail, from_tail_ref[c]))
        out_tail = out_tail + nt(mains[c], to_tail_ref[c])
    return outs, out_tail


def split_lanes(block):
    return [block[:, c * MAIN : (c + 1) * MAIN] for c in range(3)], block[:, 3 * MAIN :]


def prep_kernel(rot_ref, trans_ref, self_ref, rot_tail, *pieces):
    fold = where_one((iota((TAIL, REST), 0) % REST == iota((TAIL, REST), 1)) & (iota((TAIL, REST), 0) < 3 * REST))
    same = (iota((TAIL, TAIL), 0) // REST) == (iota((TAIL, TAIL), 1) // REST)

    def tail_block(block):
        return jnp.where(same, nt(nn(fold, block).astype(BF), fold), 0.0).astype(BF)

    for r in range(NR):
        rot_tail[r] = tail_block(rot_ref[r, MAIN:, MAIN:])
    for source, (to_tail, from_tail, tail) in ((trans_ref, pieces[:3]), (self_ref, pieces[3:])):
        for c in range(3):
            to_tail[c] = nn(spread(c), source[MAIN:, :MAIN]).astype(BF)
            from_tail[c] = nt(source[:MAIN, MAIN:], spread(c)).astype(BF)
        tail[...] = tail_block(source[MAIN:, MAIN:])


def meta_row(metas, dx, dy, row):
    return metas[dy + 1][dx + 1, row : row + 1, :]


def pick_kernel(rows, count, *refs):
    sources, metas = refs[:count], refs[count : count + 3]
    to_left, to_right = refs[count + 3 :]
    for i, (source, dy) in enumerate(zip(sources, rows)):
        for ex, out in ((-1, to_left), (1, to_right)):
            o = offset_of(-ex, dy)
            table = pick_table(meta_row(metas, ex, 0, PARTNER + o), meta_row(metas, 0, dy, OWN + 8 - o))
            for c in range(3):
                out[3 * i + c] = nn(source[c], table).astype(BF)


def phase_kernel(sources, whole, first, last, *refs):
    m = len(sources)
    arrays = refs[: (m if last is False else 2)]
    refs = refs[len(arrays) :]
    metas = refs[:3]
    rot_ref, rot_tail, trans_ref, t1, t2, t3 = refs[3:9]
    refs = refs[9:]
    if first:
        self_ref, s1, s2, s3 = refs[:4]
        refs = refs[4:]
    else:
        acc_in = refs[0]
        refs = refs[1:]
    out, picked, grouped, turned, places_to = refs[:5]
    acc = refs[5] if last else out

    def slot_rows(dx, dy, mine, theirs):
        o = offset_of(dx, dy)
        return meta_row(metas, 0, 0, mine + o), meta_row(metas, dx, dy, theirs + 8 - o)

    if first:
        unit = eye(CELLS)
        here = arrays[0]
        mains = [nt(unit, here[c, :MAIN, :]).astype(BF) for c in range(3)]
        tail = nt(unit, tail_of([here[c, MAIN:, :] for c in range(3)])).astype(BF)
        outs, out_tail = apply_dense(mains, tail, self_ref, s1, s2, s3)
        for c in range(3):
            acc[:, c * MAIN : (c + 1) * MAIN] = outs[c]
        acc[:, 3 * MAIN :] = out_tail

    rots = []
    for dx, dy in sources:
        rots.extend(slot_rows(dx, dy, ROT, ROT))
    places = positions(rots)

    for s, (dx, dy) in enumerate(sources):
        if s < whole:
            table = pick_table(*slot_rows(dx, dy, PARTNER, OWN))
            for c in range(3):
                picked[c] = nn(arrays[s][c], table).astype(BF)
            taken = [picked[c] for c in range(3)]
        elif last:
            side, which = arrays[0 if dx < 0 else 1], (0 if dy < 0 else 1)
            taken = [side[3 * which + c] for c in range(3)]
        else:
            taken = [arrays[s][c] for c in range(3)]
        row_ids = iota((ROWS, SLOTS), 0)
        own_place, partner_place = places[2 * s], places[2 * s + 1]
        place = jnp.concatenate([where_one(row_ids == own_place), where_one(row_ids == partner_place)], axis=1)
        lanes = slice(s * GROUP, (s + 1) * GROUP)
        for c in range(3):
            grouped[:, lanes, c * MAIN : (c + 1) * MAIN] = (
                nt(place, taken[c][:MAIN]).astype(BF).reshape(NR, GROUP, MAIN)
            )
        grouped[:, lanes, 3 * MAIN :] = (
            nt(place, tail_of([t[MAIN:] for t in taken])).astype(BF).reshape(NR, GROUP, TAIL)
        )
        own_to, partner_to = slot_rows(dx, dy, OWN, PARTNER)
        to = jnp.concatenate([own_to, partner_to], axis=1) + 1
        digits = jnp.concatenate([to // 32, to % 32, jnp.zeros((6, PAIR), jnp.int32)], axis=0)
        back = nt(digits.astype(F32).astype(BF), place)
        goal = (back[0:1] * 32.0 + back[1:2]).astype(jnp.int32) - 1
        places_to[:, s * ROWS : (s + 1) * ROWS] = where_one(iota((CELLS, ROWS), 0) == goal)

    size = m * GROUP
    main_signs = side_signs(MAIN, 0)
    tail_signs = side_signs(TAIL, MAIN)

    def turn(r, source, target, dot):
        block = source[r]
        mains, tail = split_lanes(block)
        turned_main = dot(jnp.concatenate(mains, axis=0), rot_ref[r, :MAIN, :MAIN])
        turned_main = (turned_main.reshape(3 * m, GROUP, MAIN) * main_signs[None]).reshape(3 * size, MAIN)
        for c in range(3):
            target[r, :, c * MAIN : (c + 1) * MAIN] = turned_main[c * size : (c + 1) * size].astype(BF)
        target[r, :, 3 * MAIN :] = dot(tail, rot_tail[r]).astype(BF)

    for r in range(NR):
        turn(r, grouped, turned, nt)

    step = 4

    def translate(i, carry):
        block = turned[pl.ds(i * step, step)].reshape(step * size, WIDE)
        mains, tail = split_lanes(block)
        outs, out_tail = apply_dense(mains, tail, trans_ref, t1, t2, t3)
        for c in range(3):
            grouped[pl.ds(i * step, step), :, c * MAIN : (c + 1) * MAIN] = (
                outs[c].astype(BF).reshape(step, size, MAIN)
            )
        grouped[pl.ds(i * step, step), :, 3 * MAIN :] = out_tail.astype(BF).reshape(step, size, TAIL)
        return carry

    lax.fori_loop(0, NR // step, translate, 0)

    for r in range(NR):
        turn(r, grouped, turned, nn)

    columns = [slice(c * MAIN, (c + 1) * MAIN) for c in range(3)] + [slice(3 * MAIN, WIDE)]
    for lanes in columns:
        total = acc[:, lanes] if first else acc_in[:, lanes]
        for s in range(m):
            back = turned[:, s * GROUP : (s + 1) * GROUP, lanes].reshape(ROWS, lanes.stop - lanes.start)
            total = total + nn(places_to[:, s * ROWS : (s + 1) * ROWS], back)
        acc[:, lanes] = total

    if last:
        unit = eye(MAIN)
        tail = acc[:, 3 * MAIN :].astype(BF)
        for c in range(3):
            out[c, :MAIN, :] = nt(unit, acc[:, c * MAIN : (c + 1) * MAIN].astype(BF)).astype(BF)
            gather = where_one(iota((REST, TAIL), 1) == iota((REST, TAIL), 0) + c * REST)
            out[c, MAIN:, :] = nt(gather, tail).astype(BF)


def vmem_call(kernel, out_shape, scratch=(), flops=0):
    return pl.pallas_call(
        kernel,
        out_shape=out_shape,
        scratch_shapes=list(scratch),
        compiler_params=pltpu.CompilerParams(vmem_limit_bytes=VMEM_LIMIT),
        cost_estimate=pl.CostEstimate(flops=flops, bytes_accessed=8_000_000, transcendentals=0),
    )


def phase_call(sources, whole, first, last):
    m = len(sources)
    if last:
        out = jax.ShapeDtypeStruct((3, K, CELLS), BF)
    else:
        out = jax.ShapeDtypeStruct((CELLS, WIDE), F32)
    scratch = [
        pltpu.VMEM((3, K, PAIR), BF),
        pltpu.VMEM((NR, m * GROUP, WIDE), BF),
        pltpu.VMEM((NR, m * GROUP, WIDE), BF),
        pltpu.VMEM((CELLS, m * ROWS), BF),
    ]
    if last:
        scratch.append(pltpu.VMEM((CELLS, WIDE), F32))
    kernel = functools.partial(phase_kernel, sources, whole, first, last)
    return vmem_call(kernel, out, scratch, flops=m * 4_000_000_000)


def shift(block, axis, distance):
    count = lax.axis_size(axis)
    return lax.ppermute(block, axis, [((i - distance) % count, i) for i in range(count)])


def local(traction, self_operator, translation, rotations, own_cell, partner_cell, rot_index, block_count):
    here = traction.reshape(3, K, CELLS)
    live = iota((9, SLOTS), 1) < block_count.reshape(9, 1)
    rot = jnp.where(live, rot_index.reshape(9, SLOTS), NR)
    meta = jnp.concatenate(
        [own_cell.reshape(9, SLOTS), partner_cell.reshape(9, SLOTS), rot, jnp.zeros((META - 27, SLOTS), jnp.int32)]
    )
    low, high = shift(here, "gy", 1), shift(here, "gy", -1)
    meta = jnp.stack([shift(meta, "gx", 1), meta, shift(meta, "gx", -1)])
    metas = (shift(meta, "gy", 1), meta, shift(meta, "gy", -1))

    picked = jax.ShapeDtypeStruct((3, K, PAIR), BF)
    to_left, to_right = vmem_call(
        functools.partial(pick_kernel, (0,), 1), (picked, picked), flops=1_000_000_000
    )(here, meta, meta, meta)
    from_left, from_right = shift(to_right, "gx", 1), shift(to_left, "gx", -1)

    dense = [
        jax.ShapeDtypeStruct((3, TAIL, MAIN), BF),
        jax.ShapeDtypeStruct((3, MAIN, TAIL), BF),
        jax.ShapeDtypeStruct((TAIL, TAIL), BF),
    ]
    rot_tail, t1, t2, t3, s1, s2, s3 = vmem_call(
        prep_kernel, [jax.ShapeDtypeStruct((NR, TAIL, TAIL), BF)] + dense + dense, flops=100_000_000
    )(rotations, translation, self_operator)
    weights = (rotations, rot_tail, translation, t1, t2, t3)

    acc = phase_call(((0, 0), (-1, 0), (1, 0)), 1, True, False)(
        here, from_left, from_right, meta, meta, meta, *weights, self_operator, s1, s2, s3
    )

    picked = jax.ShapeDtypeStruct((6, K, PAIR), BF)
    to_left, to_right = vmem_call(
        functools.partial(pick_kernel, (-1, 1), 2), (picked, picked), flops=2_000_000_000
    )(low, high, *metas)
    from_left, from_right = shift(to_right, "gx", 1), shift(to_left, "gx", -1)

    acc = phase_call(((0, -1), (0, 1)), 2, False, False)(low, high, *metas, *weights, acc)
    velocity = phase_call(((-1, -1), (-1, 1), (1, -1), (1, 1)), 0, False, True)(
        from_left, from_right, *metas, *weights, acc
    )
    return velocity.reshape(3, K, 1, 1, CELLS)


def solution(mesh):
    return jax.shard_map(
        local,
        mesh=mesh,
        in_specs=(
            P(None, None, "gx", "gy", None),
            P(),
            P(),
            P(),
            P("gx", "gy", None, None),
            P("gx", "gy", None, None),
            P("gx", "gy", None, None, None),
            P("gx", "gy", None),
        ),
        out_specs=P(None, None, "gx", "gy", None),
        check_vma=False,
    )
```

```python
import functools

import jax
import jax.numpy as jnp
from jax import lax
from jax.experimental import pallas as pl
from jax.experimental.pallas import tpu as pltpu
from jax.sharding import PartitionSpec as P

BF = jnp.bfloat16
F32 = jnp.float32

K = 289
MAIN = 256
CUT = 192
REST = K - MAIN
TAIL = 128
WIDE = 3 * MAIN + TAIL
CELLS = 512
SLOTS = 128
NR = 16
CAP = 16
PAIR = 2 * SLOTS
GROUP = 2 * CAP
ROWS = NR * GROUP
OWN, PARTNER, ROT, META = 0, 9, 18, 32
COLUMNS = (slice(0, 256), slice(256, 512), slice(512, 768), slice(768, 896))
VMEM_LIMIT = 28 * 1024 * 1024


def nt(a, b):
    return lax.dot_general(a, b, (((1,), (1,)), ((), ())), preferred_element_type=F32)


def nn(a, b):
    return jnp.dot(a, b, preferred_element_type=F32)


def iota(shape, dim):
    return lax.broadcasted_iota(jnp.int32, shape, dim)


def where_one(condition):
    return jnp.where(condition, 1.0, 0.0).astype(BF)


def eye(size):
    return where_one(iota((size, size), 0) == iota((size, size), 1))


def spread(c):
    return where_one(iota((TAIL, REST), 0) == iota((TAIL, REST), 1) + c * REST)


def offset_of(dx, dy):
    return (dx + 1) * 3 + dy + 1


def parity_lanes(width, start):
    k = iota((1, width), 1) + start
    degree = jnp.zeros((1, width), jnp.int32)
    for level in range(1, 17):
        degree = degree + jnp.where(k >= level * level, 1, 0)
    return 1.0 - 2.0 * (degree % 2).astype(F32)


def side_signs(width, start):
    signs = jnp.broadcast_to(parity_lanes(width, start), (GROUP, width))
    return jnp.where(iota((GROUP, width), 0) >= CAP, signs, 1.0)


def pick_table(own_side, partner_side):
    cells = iota((CELLS, SLOTS), 0)
    return jnp.concatenate([where_one(cells == own_side), where_one(cells == partner_side)], axis=1)


def tail_of(parts):
    total = None
    for c, part in enumerate(parts):
        term = nn(spread(c), part)
        total = term if total is None else total + term
    return total.astype(BF)


def positions(rots):
    marks = [where_one(iota((NR, SLOTS), 0) == rot) for rot in rots]
    earlier = where_one(iota((SLOTS, SLOTS), 0) < iota((SLOTS, SLOTS), 1))
    ranks = nn(jnp.concatenate(marks, axis=0), earlier)
    places = []
    for j, mark in enumerate(marks):
        base = (iota((NR, SLOTS), 0) * GROUP + (j % 2) * CAP + 1).astype(F32)
        values = mark.astype(F32) * (ranks[j * NR : (j + 1) * NR] + base)
        places.append(jnp.sum(values, axis=0, keepdims=True).astype(jnp.int32) - 1)
    return places


def apply_dense(block, main_ref, tail_ref):
    tail = block[:, 3 * MAIN :]
    outs = [
        nt(jnp.concatenate([block[:, c * MAIN : (c + 1) * MAIN], tail], axis=1), main_ref[c]) for c in range(3)
    ]
    return outs + [nt(block, tail_ref[...])]


def split_lanes(block):
    return [block[:, c * MAIN : (c + 1) * MAIN] for c in range(3)], block[:, 3 * MAIN :]


def prep_kernel(rot_ref, trans_ref, self_ref, rot_tail, *pieces):
    fold = where_one((iota((TAIL, REST), 0) % REST == iota((TAIL, REST), 1)) & (iota((TAIL, REST), 0) < 3 * REST))
    same = (iota((TAIL, TAIL), 0) // REST) == (iota((TAIL, TAIL), 1) // REST)

    def tail_block(block):
        return jnp.where(same, nt(nn(fold, block).astype(BF), fold), 0.0).astype(BF)

    for r in range(NR):
        rot_tail[r] = tail_block(rot_ref[r, MAIN:, MAIN:])
    for source, (main, tail) in ((trans_ref, pieces[:2]), (self_ref, pieces[2:])):
        for c in range(3):
            main[c, :, :MAIN] = source[:MAIN, :MAIN]
            main[c, :, MAIN:] = nt(source[:MAIN, MAIN:], spread(c)).astype(BF)
            tail[:, c * MAIN : (c + 1) * MAIN] = nn(spread(c), source[MAIN:, :MAIN]).astype(BF)
        tail[:, 3 * MAIN :] = tail_block(source[MAIN:, MAIN:])


def meta_row(metas, dx, dy, row):
    meta = metas[dy + 1]
    return meta[dx + 1 if meta.shape[0] == 3 else 0, row : row + 1, :]


def pick_kernel(rows, count, *refs):
    sources, metas = refs[:count], refs[count : count + 3]
    to_left, to_right = refs[count + 3 :]
    for i, (source, dy) in enumerate(zip(sources, rows)):
        for ex, out in ((-1, to_left), (1, to_right)):
            o = offset_of(-ex, dy)
            table = pick_table(meta_row(metas, ex, 0, PARTNER + o), meta_row(metas, 0, dy, OWN + 8 - o))
            for c in range(3):
                out[3 * i + c] = nn(source[c], table).astype(BF)


def column_source(kind, arrays, s, dx, dy):
    if kind == "here":
        return [[arrays[0][c]] for c in range(3)]
    if kind == "sides":
        return [[arrays[s][c]] for c in range(3)]
    if kind == "rows":
        return [[arrays[2 * s][c], arrays[2 * s + 1][c]] for c in range(3)]
    low, high = arrays[:2] if dx < 0 else arrays[2:]
    which = 0 if dy < 0 else 3
    return [[low[which + c], high[which + c]] for c in range(3)]


PHASES = {
    "here": (((0, 0),), 1),
    "sides": (((-1, 0), (1, 0)), 2),
    "rows": (((0, -1), (0, 1)), 4),
    "corners": (((-1, -1), (-1, 1), (1, -1), (1, 1)), 4),
}


def phase_kernel(kind, *refs):
    sources, inputs = PHASES[kind]
    first, last, whole = kind == "here", kind == "corners", kind in ("here", "rows")
    m = len(sources)
    arrays, refs = refs[:inputs], refs[inputs:]
    metas = refs[:3]
    rot_ref, rot_tail, trans_main, trans_tail = refs[3:7]
    refs = refs[7:]
    if first:
        self_main, self_tail = refs[:2]
        refs = refs[2:]
    else:
        acc_in = refs[0]
        refs = refs[1:]
    out, picked, grouped, turned, places_to = refs[:5]
    acc = refs[5] if last else out

    def slot_rows(dx, dy, mine, theirs):
        o = offset_of(dx, dy)
        return meta_row(metas, 0, 0, mine + o), meta_row(metas, dx, dy, theirs + 8 - o)

    if first:
        unit = eye(CELLS)
        here = arrays[0]
        parts = [nt(unit, here[c, :MAIN, :]).astype(BF) for c in range(3)]
        parts.append(nt(unit, tail_of([here[c, MAIN:, :] for c in range(3)])).astype(BF))
        for lanes, part in zip(COLUMNS, apply_dense(jnp.concatenate(parts, axis=1), self_main, self_tail)):
            acc[:, lanes] = part

    rots = []
    for dx, dy in sources:
        rots.extend(slot_rows(dx, dy, ROT, ROT))
    places = positions(rots)

    for s, (dx, dy) in enumerate(sources):
        taken = column_source(kind, arrays, s, dx, dy)
        if whole:
            table = pick_table(*slot_rows(dx, dy, PARTNER, OWN))
            for c in range(3):
                start = 0
                for piece in taken[c]:
                    picked[c, start : start + piece.shape[0]] = nn(piece, table).astype(BF)
                    start += piece.shape[0]
            taken = [picked[c] for c in range(3)]
        else:
            taken = [jnp.concatenate(pieces, axis=0) for pieces in taken]
        row_ids = iota((ROWS, SLOTS), 0)
        own_place, partner_place = places[2 * s], places[2 * s + 1]
        place = jnp.concatenate([where_one(row_ids == own_place), where_one(row_ids == partner_place)], axis=1)
        lanes = slice(s * GROUP, (s + 1) * GROUP)
        for c in range(3):
            grouped[:, lanes, c * MAIN : (c + 1) * MAIN] = (
                nt(place, taken[c][:MAIN]).astype(BF).reshape(NR, GROUP, MAIN)
            )
        grouped[:, lanes, 3 * MAIN :] = (
            nt(place, tail_of([t[MAIN:] for t in taken])).astype(BF).reshape(NR, GROUP, TAIL)
        )
        own_to, partner_to = slot_rows(dx, dy, OWN, PARTNER)
        to = jnp.concatenate([own_to, partner_to], axis=1) + 1
        digits = jnp.concatenate([to // 32, to % 32, jnp.zeros((6, PAIR), jnp.int32)], axis=0)
        back = nt(digits.astype(F32).astype(BF), place)
        goal = (back[0:1] * 32.0 + back[1:2]).astype(jnp.int32) - 1
        places_to[:, s * ROWS : (s + 1) * ROWS] = where_one(iota((CELLS, ROWS), 0) == goal)

    size = m * GROUP
    main_signs = side_signs(MAIN, 0)
    tail_signs = side_signs(TAIL, MAIN)

    def turn(r, source, target, dot):
        block = source[r]
        mains, tail = split_lanes(block)
        turned_main = dot(jnp.concatenate(mains, axis=0), rot_ref[r, :MAIN, :MAIN])
        turned_main = (turned_main.reshape(3 * m, GROUP, MAIN) * main_signs[None]).reshape(3 * size, MAIN)
        for c in range(3):
            target[r, :, c * MAIN : (c + 1) * MAIN] = turned_main[c * size : (c + 1) * size].astype(BF)
        target[r, :, 3 * MAIN :] = dot(tail, rot_tail[r]).astype(BF)

    for r in range(NR):
        turn(r, grouped, turned, nt)

    block = turned[...].reshape(NR * size, WIDE)
    for lanes, part in zip(COLUMNS, apply_dense(block, trans_main, trans_tail)):
        grouped[:, :, lanes] = part.astype(BF).reshape(NR, size, lanes.stop - lanes.start)

    for r in range(NR):
        turn(r, grouped, turned, nn)

    for lanes in COLUMNS:
        width = lanes.stop - lanes.start
        back = [turned[:, s * GROUP : (s + 1) * GROUP, lanes].reshape(ROWS, width) for s in range(m)]
        total = nn(places_to[...], jnp.concatenate(back, axis=0))
        acc[:, lanes] = total + (acc[:, lanes] if first else acc_in[:, lanes])

    if last:
        unit = eye(MAIN)
        tail = acc[:, 3 * MAIN :].astype(BF)
        for c in range(3):
            out[c, :MAIN, :] = nt(unit, acc[:, c * MAIN : (c + 1) * MAIN].astype(BF)).astype(BF)
            gather = where_one(iota((REST, TAIL), 1) == iota((REST, TAIL), 0) + c * REST)
            out[c, MAIN:, :] = nt(gather, tail).astype(BF)


def vmem_call(kernel, out_shape, scratch=(), flops=0):
    return pl.pallas_call(
        kernel,
        out_shape=out_shape,
        scratch_shapes=list(scratch),
        compiler_params=pltpu.CompilerParams(vmem_limit_bytes=VMEM_LIMIT),
        cost_estimate=pl.CostEstimate(flops=flops, bytes_accessed=8_000_000, transcendentals=0),
    )


def phase_call(kind):
    m, last = len(PHASES[kind][0]), kind == "corners"
    if last:
        out = jax.ShapeDtypeStruct((3, K, CELLS), BF)
    else:
        out = jax.ShapeDtypeStruct((CELLS, WIDE), F32)
    scratch = [
        pltpu.VMEM((3, K, PAIR), BF),
        pltpu.VMEM((NR, m * GROUP, WIDE), BF),
        pltpu.VMEM((NR, m * GROUP, WIDE), BF),
        pltpu.VMEM((CELLS, m * ROWS), BF),
    ]
    if last:
        scratch.append(pltpu.VMEM((CELLS, WIDE), F32))
    kernel = functools.partial(phase_kernel, kind)
    return vmem_call(kernel, out, scratch, flops=m * 4_000_000_000)


def shift(block, axis, distance):
    count = lax.axis_size(axis)
    return lax.ppermute(block, axis, [((i - distance) % count, i) for i in range(count)])


def local(traction, self_operator, translation, rotations, own_cell, partner_cell, rot_index, block_count):
    here = traction.reshape(3, K, CELLS)
    live = iota((9, SLOTS), 1) < block_count.reshape(9, 1)
    rot = jnp.where(live, rot_index.reshape(9, SLOTS), NR)
    meta = jnp.concatenate(
        [own_cell.reshape(9, SLOTS), partner_cell.reshape(9, SLOTS), rot, jnp.zeros((META - 27, SLOTS), jnp.int32)]
    )
    low_a, high_a = shift(here[:, :CUT], "gy", 1), shift(here[:, :CUT], "gy", -1)
    low_b, high_b = shift(here[:, CUT:], "gy", 1), shift(here[:, CUT:], "gy", -1)
    mine = meta[None]
    meta = jnp.stack([shift(meta, "gx", 1), meta, shift(meta, "gx", -1)])
    meta_low, meta_high = shift(meta, "gy", 1), shift(meta, "gy", -1)

    dense = [
        jax.ShapeDtypeStruct((3, MAIN, MAIN + TAIL), BF),
        jax.ShapeDtypeStruct((TAIL, WIDE), BF),
    ]
    rot_tail, *dense = vmem_call(
        prep_kernel, [jax.ShapeDtypeStruct((NR, TAIL, TAIL), BF)] + dense + dense, flops=100_000_000
    )(rotations, translation, self_operator)
    weights = (rotations, rot_tail, *dense[:2])

    def pick(sources, rows, metas):
        picked = jax.ShapeDtypeStruct((3 * len(rows), sources[0].shape[1], PAIR), BF)
        to_left, to_right = vmem_call(
            functools.partial(pick_kernel, rows, len(rows)), (picked, picked), flops=1_000_000_000
        )(*sources, *metas)
        return to_left, shift(to_right, "gx", 1), shift(to_left, "gx", -1)

    after = lax.optimization_barrier
    acc = phase_call("here")(here, mine, mine, mine, *weights, *dense[2:])
    meta, meta_low, meta_high, acc = after((meta, meta_low, meta_high, acc))
    _, from_left, from_right = pick((here,), (0,), (meta, meta, meta))
    done, left_a, right_a = pick((low_a, high_a), (-1, 1), (meta_low, meta, meta_high))
    meta, done = after((meta, done))
    acc = phase_call("sides")(from_left, from_right, meta, meta, meta, *weights, acc)
    meta_low, meta_high, acc = after((meta_low, meta_high, acc))
    done, left_b, right_b = pick((low_b, high_b), (-1, 1), (meta_low, meta, meta_high))
    meta, done = after((meta, done))
    metas = (meta_low, meta, meta_high)
    acc = phase_call("rows")(low_a, low_b, high_a, high_b, *metas, *weights, acc)
    velocity = phase_call("corners")(left_a, left_b, right_a, right_b, *metas, *weights, acc)
    return velocity.reshape(3, K, 1, 1, CELLS)


def solution(mesh):
    return jax.shard_map(
        local,
        mesh=mesh,
        in_specs=(
            P(None, None, "gx", "gy", None),
            P(),
            P(),
            P(),
            P("gx", "gy", None, None),
            P("gx", "gy", None, None),
            P("gx", "gy", None, None, None),
            P("gx", "gy", None),
        ),
        out_specs=P(None, None, "gx", "gy", None),
        check_vma=False,
    )
```

```python
import functools

import jax
import jax.numpy as jnp
from jax import lax
from jax.experimental import pallas as pl
from jax.experimental.pallas import tpu as pltpu
from jax.sharding import PartitionSpec as P

BF = jnp.bfloat16
F32 = jnp.float32

K = 289
MAIN = 256
REST = K - MAIN
TAIL = 128
WIDE = 3 * MAIN + TAIL
CELLS = 512
SLOTS = 128
NR = 16
CAP = 16
PAIR = 2 * SLOTS
GROUP = 2 * CAP
ROWS = NR * GROUP
HEAD = 16
BASE = 32
OWN, PARTNER, ROT = 0, 2, 4
COLUMNS = (slice(0, 256), slice(256, 512), slice(512, 768), slice(768, 896))
VMEM_LIMIT = 28 * 1024 * 1024
PACK_LIMIT = 62 * 1024 * 1024


def nt(a, b):
    return lax.dot_general(a, b, (((1,), (1,)), ((), ())), preferred_element_type=F32)


def nn(a, b):
    return jnp.dot(a, b, preferred_element_type=F32)


def iota(shape, dim):
    return lax.broadcasted_iota(jnp.int32, shape, dim)


def where_one(condition):
    return jnp.where(condition, 1.0, 0.0).astype(BF)


def eye(size):
    return where_one(iota((size, size), 0) == iota((size, size), 1))


def spread(c):
    return where_one(iota((TAIL, REST), 0) == iota((TAIL, REST), 1) + c * REST)


def offset_of(dx, dy):
    return (dx + 1) * 3 + dy + 1


def parity_lanes(width, start):
    k = iota((1, width), 1) + start
    degree = jnp.zeros((1, width), jnp.int32)
    for level in range(1, 17):
        degree = degree + jnp.where(k >= level * level, 1, 0)
    return 1.0 - 2.0 * (degree % 2).astype(F32)


def side_signs(width, start):
    signs = jnp.broadcast_to(parity_lanes(width, start), (GROUP, width))
    return jnp.where(iota((GROUP, width), 0) >= CAP, signs, 1.0)


def pick_table(own_side, partner_side):
    cells = iota((CELLS, SLOTS), 0)
    return jnp.concatenate([where_one(cells == own_side), where_one(cells == partner_side)], axis=1)


def tail_of(parts):
    total = None
    for c, part in enumerate(parts):
        term = nn(spread(c), part)
        total = term if total is None else total + term
    return total.astype(BF)


def positions(rots):
    marks = [where_one(iota((NR, SLOTS), 0) == rot) for rot in rots]
    earlier = where_one(iota((SLOTS, SLOTS), 0) < iota((SLOTS, SLOTS), 1))
    ranks = nn(jnp.concatenate(marks, axis=0), earlier)
    places = []
    for j, mark in enumerate(marks):
        base = (iota((NR, SLOTS), 0) * GROUP + (j % 2) * CAP + 1).astype(F32)
        values = mark.astype(F32) * (ranks[j * NR : (j + 1) * NR] + base)
        places.append(jnp.sum(values, axis=0, keepdims=True).astype(jnp.int32) - 1)
    return places


def apply_dense(block, main_ref, tail_ref):
    tail = block[:, 3 * MAIN :]
    outs = [
        nt(jnp.concatenate([block[:, c * MAIN : (c + 1) * MAIN], tail], axis=1), main_ref[c]) for c in range(3)
    ]
    return outs + [nt(block, tail_ref[...])]


def split_lanes(block):
    return [block[:, c * MAIN : (c + 1) * MAIN] for c in range(3)], block[:, 3 * MAIN :]


def prep_kernel(rot_ref, trans_ref, self_ref, rot_tail, *pieces):
    fold = where_one((iota((TAIL, REST), 0) % REST == iota((TAIL, REST), 1)) & (iota((TAIL, REST), 0) < 3 * REST))
    same = (iota((TAIL, TAIL), 0) // REST) == (iota((TAIL, TAIL), 1) // REST)

    def tail_block(block):
        return jnp.where(same, nt(nn(fold, block).astype(BF), fold), 0.0).astype(BF)

    for r in range(NR):
        rot_tail[r] = tail_block(rot_ref[r, MAIN:, MAIN:])
    for source, (main, tail) in ((trans_ref, pieces[:2]), (self_ref, pieces[2:])):
        for c in range(3):
            main[c, :, :MAIN] = source[:MAIN, :MAIN]
            main[c, :, MAIN:] = nt(source[:MAIN, MAIN:], spread(c)).astype(BF)
            tail[:, c * MAIN : (c + 1) * MAIN] = nn(spread(c), source[MAIN:, :MAIN]).astype(BF)
        tail[:, 3 * MAIN :] = tail_block(source[MAIN:, MAIN:])


def head_row(ref, first, what, row):
    def part(number):
        lanes = slice(number % 4 * SLOTS, (number % 4 + 1) * SLOTS)
        return ref[first + number // 4, :HEAD, lanes].astype(F32)[row : row + 1]

    if what == ROT:
        return part(ROT).astype(jnp.int32)
    return (part(what) * BASE + part(what + 1)).astype(jnp.int32)


def head_digits(index):
    high = index // BASE
    return high.astype(F32).astype(BF), (index - high * BASE).astype(F32).astype(BF)


def pack_kernel(*refs):
    sources, out, held, done = refs[:5], refs[5], refs[6:11], refs[11]
    copies = [pltpu.make_async_copy(src, dst, done.at[i]) for i, (src, dst) in enumerate(zip(sources, held))]
    for copy in copies:
        copy.start()
    for copy in copies:
        copy.wait()
    count_ref, own_ref, partner_ref, rot_ref, here_ref = held
    empty = [jnp.zeros((HEAD - 9, SLOTS), jnp.int32)]
    own = jnp.concatenate([own_ref[o] for o in range(9)] + empty, axis=0)
    partner = jnp.concatenate([partner_ref[o] for o in range(9)] + empty, axis=0)
    slot = iota((1, SLOTS), 1)
    live = [jnp.where(slot < count_ref[0, o], rot_ref[o], NR) for o in range(9)]
    rot = jnp.concatenate(live + empty, axis=0).astype(F32).astype(BF)
    out[0, :HEAD, :] = jnp.concatenate(head_digits(own) + head_digits(partner), axis=1)
    out[1, :HEAD, :] = jnp.concatenate([rot, jnp.zeros((HEAD, CELLS - SLOTS), BF)], axis=1)
    out[2, :HEAD, :] = jnp.zeros((HEAD, CELLS), BF)
    for c in range(3):
        out[c, HEAD:, :] = here_ref[c]


def pick_kernel(left, right, high, low, to_left, to_right):
    for i, (source, dy) in enumerate(((low, -1), (high, 1))):
        for ex, target, out in ((-1, left, to_left), (1, right, to_right)):
            o = offset_of(-ex, dy)
            table = pick_table(head_row(target, 0, PARTNER, o), head_row(source, 0, OWN, 8 - o))
            for c in range(3):
                out[3 * i + c, HEAD:, :] = nn(source[c, HEAD:, :], table).astype(BF)
            digits = [jnp.broadcast_to(d, (HEAD, SLOTS)) for d in head_digits(head_row(source, 0, PARTNER, 8 - o))]
            rot = jnp.broadcast_to(head_row(source, 0, ROT, 8 - o).astype(F32).astype(BF), (HEAD, SLOTS))
            out[3 * i, :HEAD, :] = jnp.concatenate(digits, axis=1)
            out[3 * i + 1, :HEAD, :] = jnp.concatenate([rot, rot], axis=1)
            out[3 * i + 2, :HEAD, :] = jnp.zeros((HEAD, PAIR), BF)


PHASES = {
    "line": ((0, 0), (-1, 0), (1, 0)),
    "rows": ((0, -1), (0, 1)),
    "corners": ((-1, -1), (-1, 1), (1, -1), (1, 1)),
}


def phase_kernel(kind, *refs):
    sources = PHASES[kind]
    first, last = kind == "line", kind == "corners"
    m = len(sources)
    mine, refs = refs[0], refs[1:]
    arrays, refs = refs[:2], refs[2:]
    if first:
        arrays = (mine, *arrays)
    rot_ref, rot_tail, trans_main, trans_tail = refs[:4]
    refs = refs[4:]
    if first:
        self_main, self_tail = refs[:2]
        refs = refs[2:]
    else:
        acc_in = refs[0]
        refs = refs[1:]
    out, picked, grouped, turned, places_to = refs[:5]
    acc = refs[5] if last else out

    def place_of(s):
        dx, dy = sources[s]
        o = offset_of(dx, dy)
        if last:
            return arrays[0 if dx < 0 else 1], (0 if dy < 0 else 3), o, 0
        return arrays[s], 0, o, 8 - o

    def slot_pair(s, mine_what, their_what):
        array, start, o, row = place_of(s)
        if last and their_what == PARTNER:
            their_what = OWN
        return head_row(mine, 0, mine_what, o), head_row(array, start, their_what, row)

    if first:
        unit = eye(CELLS)
        parts = [nt(unit, mine[c, HEAD : HEAD + MAIN, :]).astype(BF) for c in range(3)]
        parts.append(nt(unit, tail_of([mine[c, HEAD + MAIN :, :] for c in range(3)])).astype(BF))
        for lanes, part in zip(COLUMNS, apply_dense(jnp.concatenate(parts, axis=1), self_main, self_tail)):
            acc[:, lanes] = part

    rots = []
    for s in range(m):
        rots.extend(slot_pair(s, ROT, ROT))
    places = positions(rots)

    for s in range(m):
        array, start = place_of(s)[:2]
        taken = [array[start + c, HEAD:, :] for c in range(3)]
        if not last:
            table = pick_table(*slot_pair(s, PARTNER, OWN))
            for c in range(3):
                picked[c] = nn(taken[c], table).astype(BF)
            taken = [picked[c] for c in range(3)]
        row_ids = iota((ROWS, SLOTS), 0)
        own_place, partner_place = places[2 * s], places[2 * s + 1]
        place = jnp.concatenate([where_one(row_ids == own_place), where_one(row_ids == partner_place)], axis=1)
        lanes = slice(s * GROUP, (s + 1) * GROUP)
        for c in range(3):
            grouped[:, lanes, c * MAIN : (c + 1) * MAIN] = (
                nt(place, taken[c][:MAIN]).astype(BF).reshape(NR, GROUP, MAIN)
            )
        grouped[:, lanes, 3 * MAIN :] = (
            nt(place, tail_of([t[MAIN:] for t in taken])).astype(BF).reshape(NR, GROUP, TAIL)
        )
        own_to, partner_to = slot_pair(s, OWN, PARTNER)
        to = jnp.concatenate([own_to, partner_to], axis=1) + 1
        digits = jnp.concatenate([to // BASE, to % BASE, jnp.zeros((6, PAIR), jnp.int32)], axis=0)
        back = nt(digits.astype(F32).astype(BF), place)
        goal = (back[0:1] * BASE + back[1:2]).astype(jnp.int32) - 1
        places_to[:, s * ROWS : (s + 1) * ROWS] = where_one(iota((CELLS, ROWS), 0) == goal)

    size = m * GROUP
    main_signs = side_signs(MAIN, 0)
    tail_signs = side_signs(TAIL, MAIN)

    def turn(r, source, target, dot):
        block = source[r]
        mains, tail = split_lanes(block)
        turned_main = dot(jnp.concatenate(mains, axis=0), rot_ref[r, :MAIN, :MAIN])
        turned_main = (turned_main.reshape(3 * m, GROUP, MAIN) * main_signs[None]).reshape(3 * size, MAIN)
        for c in range(3):
            target[r, :, c * MAIN : (c + 1) * MAIN] = turned_main[c * size : (c + 1) * size].astype(BF)
        target[r, :, 3 * MAIN :] = dot(tail, rot_tail[r]).astype(BF)

    for r in range(NR):
        turn(r, grouped, turned, nt)

    block = turned[...].reshape(NR * size, WIDE)
    for lanes, part in zip(COLUMNS, apply_dense(block, trans_main, trans_tail)):
        grouped[:, :, lanes] = part.astype(BF).reshape(NR, size, lanes.stop - lanes.start)

    for r in range(NR):
        turn(r, grouped, turned, nn)

    for lanes in COLUMNS:
        width = lanes.stop - lanes.start
        back = [turned[:, s * GROUP : (s + 1) * GROUP, lanes].reshape(ROWS, width) for s in range(m)]
        total = nn(places_to[...], jnp.concatenate(back, axis=0))
        acc[:, lanes] = total + (acc[:, lanes] if first else acc_in[:, lanes])

    if last:
        unit = eye(MAIN)
        tail = acc[:, 3 * MAIN :].astype(BF)
        for c in range(3):
            out[c, :MAIN, :] = nt(unit, acc[:, c * MAIN : (c + 1) * MAIN].astype(BF)).astype(BF)
            gather = where_one(iota((REST, TAIL), 1) == iota((REST, TAIL), 0) + c * REST)
            out[c, MAIN:, :] = nt(gather, tail).astype(BF)


def vmem_call(kernel, out_shape, scratch=(), limit=VMEM_LIMIT, **options):
    return pl.pallas_call(
        kernel,
        out_shape=out_shape,
        scratch_shapes=list(scratch),
        compiler_params=pltpu.CompilerParams(vmem_limit_bytes=limit),
        cost_estimate=pl.CostEstimate(flops=1000, bytes_accessed=1000, transcendentals=0),
        **options,
    )


def phase_call(kind):
    m, last = len(PHASES[kind]), kind == "corners"
    if last:
        out = jax.ShapeDtypeStruct((3, K, CELLS), BF)
    else:
        out = jax.ShapeDtypeStruct((CELLS, WIDE), F32)
    scratch = [
        pltpu.VMEM((3, K, PAIR), BF),
        pltpu.VMEM((NR, m * GROUP, WIDE), BF),
        pltpu.VMEM((NR, m * GROUP, WIDE), BF),
        pltpu.VMEM((CELLS, m * ROWS), BF),
    ]
    if last:
        scratch.append(pltpu.VMEM((CELLS, WIDE), F32))
    kernel = functools.partial(phase_kernel, kind)
    return vmem_call(kernel, out, scratch)


def shift(block, axis, distance):
    count = lax.axis_size(axis)
    return lax.ppermute(block, axis, [((i - distance) % count, i) for i in range(count)])


def local(traction, self_operator, translation, rotations, own_cell, partner_cell, rot_index, block_count):
    here = traction.reshape(3, K, CELLS)
    slots = [a.reshape(9, 1, SLOTS) for a in (own_cell, partner_cell, rot_index)]
    mine = vmem_call(
        pack_kernel,
        jax.ShapeDtypeStruct((3, HEAD + K, CELLS), BF),
        [pltpu.SMEM((1, 9), jnp.int32)]
        + [pltpu.VMEM((9, 1, SLOTS), jnp.int32)] * 3
        + [pltpu.VMEM((3, K, CELLS), BF), pltpu.SemaphoreType.DMA((5,))],
        limit=PACK_LIMIT,
        in_specs=[pl.BlockSpec(memory_space=pl.ANY)] * 5,
    )(block_count.reshape(1, 9), *slots, here)
    left, right = shift(mine, "gx", 1), shift(mine, "gx", -1)
    high = shift(mine, "gy", -1)
    low = shift(mine, "gy", 1)
    after = lax.optimization_barrier

    dense = [
        jax.ShapeDtypeStruct((3, MAIN, MAIN + TAIL), BF),
        jax.ShapeDtypeStruct((TAIL, WIDE), BF),
    ]
    rot_tail, *dense = vmem_call(
        prep_kernel, [jax.ShapeDtypeStruct((NR, TAIL, TAIL), BF)] + dense + dense
    )(rotations, translation, self_operator)
    weights = (rotations, rot_tail, *dense[:2])

    acc = phase_call("line")(mine, left, right, *weights, *dense[2:])
    acc, high, low = after((acc, high, low))
    picked = jax.ShapeDtypeStruct((6, HEAD + K, PAIR), BF)
    to_left, to_right = vmem_call(pick_kernel, (picked, picked))(left, right, high, low)
    far_left, far_right = shift(to_right, "gx", 1), shift(to_left, "gx", -1)
    to_left, high, low = after((to_left, high, low))
    acc = phase_call("rows")(mine, low, high, *weights, acc)
    velocity = phase_call("corners")(mine, far_left, far_right, *weights, acc)
    return velocity.reshape(3, K, 1, 1, CELLS)


def solution(mesh):
    return jax.shard_map(
        local,
        mesh=mesh,
        in_specs=(
            P(None, None, "gx", "gy", None),
            P(),
            P(),
            P(),
            P("gx", "gy", None, None),
            P("gx", "gy", None, None),
            P("gx", "gy", None, None, None),
            P("gx", "gy", None),
        ),
        out_specs=P(None, None, "gx", "gy", None),
        check_vma=False,
    )
```

```python
import functools

import jax
import jax.numpy as jnp
from jax import lax
from jax.experimental import pallas as pl
from jax.experimental.pallas import tpu as pltpu
from jax.sharding import PartitionSpec as P

BF = jnp.bfloat16
F32 = jnp.float32

K = 289
MAIN = 256
REST = K - MAIN
TAIL = 128
WIDE = 3 * MAIN + TAIL
CELLS = 512
SLOTS = 128
NR = 16
CAP = 16
PAIR = 2 * SLOTS
GROUP = 2 * CAP
ROWS = NR * GROUP
HEAD = 16
HEAD_AT = WIDE - HEAD
BASE = 32
OWN, PARTNER = 0, 2
ROT = 9
ODD = 12
COLUMNS = (slice(0, 256), slice(256, 512), slice(512, 768), slice(768, 896))
VMEM_LIMIT = 28 * 1024 * 1024
HERE_COST = 30_000_000_000
PACK_LIMIT = 62 * 1024 * 1024


def nt(a, b):
    return lax.dot_general(a, b, (((1,), (1,)), ((), ())), preferred_element_type=F32)


def nn(a, b):
    return jnp.dot(a, b, preferred_element_type=F32)


def iota(shape, dim):
    return lax.broadcasted_iota(jnp.int32, shape, dim)


def where_one(condition):
    return jnp.where(condition, 1.0, 0.0).astype(BF)


def eye(size):
    return where_one(iota((size, size), 0) == iota((size, size), 1))


def spread(c):
    return where_one(iota((TAIL, REST), 0) == iota((TAIL, REST), 1) + c * REST)


def offset_of(dx, dy):
    return (dx + 1) * 3 + dy + 1


def offsets(side, dy):
    return offset_of(side, dy), offset_of(-side, dy)


def choose(even, side, dy, read, theirs=False):
    first, second = [8 - o if theirs else o for o in offsets(side, dy)]
    return read(first) if first == second else jnp.where(even, read(first), read(second))


def parity_lanes(width, start):
    k = iota((1, width), 1) + start
    degree = jnp.zeros((1, width), jnp.int32)
    for level in range(1, 17):
        degree = degree + jnp.where(k >= level * level, 1, 0)
    return 1.0 - 2.0 * (degree % 2).astype(F32)


def side_signs(width, start):
    signs = jnp.broadcast_to(parity_lanes(width, start), (GROUP, width))
    return jnp.where(iota((GROUP, width), 0) >= CAP, signs, 1.0)


def pick_table(own_side, partner_side):
    cells = iota((CELLS, SLOTS), 0)
    return jnp.concatenate([where_one(cells == own_side), where_one(cells == partner_side)], axis=1)


def positions(rots):
    marks = [where_one(iota((NR, SLOTS), 0) == rot) for rot in rots]
    earlier = where_one(iota((SLOTS, SLOTS), 0) < iota((SLOTS, SLOTS), 1))
    ranks = nn(jnp.concatenate(marks, axis=0), earlier)
    places = []
    for j, mark in enumerate(marks):
        base = (iota((NR, SLOTS), 0) * GROUP + (j % 2) * CAP + 1).astype(F32)
        values = mark.astype(F32) * (ranks[j * NR : (j + 1) * NR] + base)
        places.append(jnp.sum(values, axis=0, keepdims=True).astype(jnp.int32) - 1)
    return places


def apply_dense(block, main_ref, tail_ref):
    tail = block[:, 3 * MAIN :]
    outs = [
        nt(jnp.concatenate([block[:, c * MAIN : (c + 1) * MAIN], tail], axis=1), main_ref[c]) for c in range(3)
    ]
    return outs + [nt(block, tail_ref[...])]


def split_lanes(block):
    return [block[:, c * MAIN : (c + 1) * MAIN] for c in range(3)], block[:, 3 * MAIN :]


def prep_kernel(rot_ref, trans_ref, self_ref, rot_tail, *pieces):
    fold = where_one((iota((TAIL, REST), 0) % REST == iota((TAIL, REST), 1)) & (iota((TAIL, REST), 0) < 3 * REST))
    same = (iota((TAIL, TAIL), 0) // REST) == (iota((TAIL, TAIL), 1) // REST)

    def tail_block(block):
        return jnp.where(same, nt(nn(fold, block).astype(BF), fold), 0.0).astype(BF)

    for r in range(NR):
        rot_tail[r] = tail_block(rot_ref[r, MAIN:, MAIN:])
    for source, (main, tail) in ((trans_ref, pieces[:2]), (self_ref, pieces[2:])):
        for c in range(3):
            main[c, :, :MAIN] = source[:MAIN, :MAIN]
            main[c, :, MAIN:] = nt(source[:MAIN, MAIN:], spread(c)).astype(BF)
            tail[:, c * MAIN : (c + 1) * MAIN] = nn(spread(c), source[MAIN:, :MAIN]).astype(BF)
        tail[:, 3 * MAIN :] = tail_block(source[MAIN:, MAIN:])


def head_part(ref, at, row, block):
    lanes = slice(block * SLOTS, (block + 1) * SLOTS)
    return ref[at : at + HEAD, lanes].astype(F32)[row : row + 1]


def head_cells(ref, what, row, at=HEAD_AT):
    return (head_part(ref, at, row, what) * BASE + head_part(ref, at, row, what + 1)).astype(jnp.int32)


def head_rots(ref, o):
    return head_part(ref, HEAD_AT, ROT + o // 4, o % 4).astype(jnp.int32)


def is_even(mine):
    return head_part(mine, HEAD_AT, ODD, 0) < 0.5


def head_digits(index):
    high = index // BASE
    return high.astype(F32).astype(BF), (index - high * BASE).astype(F32).astype(BF)


def pack_kernel(count_ref, own_ref, partner_ref, rot_ref, here_ref, out, *scratch):
    held, tail, arrived, sent = scratch[:5], scratch[5], scratch[6], scratch[7]
    copies = [
        pltpu.make_async_copy(src, dst, arrived.at[i])
        for i, (src, dst) in enumerate(zip((count_ref, own_ref, partner_ref, rot_ref, here_ref), held))
    ]
    for copy in copies:
        copy.start()
    for copy in copies:
        copy.wait()
    count, own, partner, rot, here = held
    mains = [
        pltpu.make_async_copy(here.at[c, :MAIN], out.at[c * MAIN : (c + 1) * MAIN], sent.at[c]) for c in range(3)
    ]
    for copy in mains:
        copy.start()
    rest = nn(spread(0), here[0, MAIN:]) + nn(spread(1), here[1, MAIN:]) + nn(spread(2), here[2, MAIN:])
    tail[...] = rest.astype(BF)
    cells = [jnp.concatenate([ref[o] for o in range(9)], axis=0) for ref in (own, partner)]
    digits = jnp.concatenate([d.astype(F32) for index in cells for d in head_digits(index)], axis=1)
    slot = iota((1, SLOTS), 1)
    live = [jnp.where(slot < count[0, o], rot[o], NR).astype(F32) for o in range(9)]
    live.extend([jnp.zeros((1, SLOTS), F32)] * 3)
    rots = [jnp.concatenate(live[4 * i : 4 * i + 4], axis=1) for i in range(3)]
    odd = lax.rem(lax.axis_index("gx"), 2)
    rows = iota((HEAD - ODD, CELLS), 0)
    flags = jnp.where((rows == 0) & (rows + odd > 0), 1.0, 0.0)
    tail[TAIL - HEAD :] = jnp.concatenate([digits, *rots, flags], axis=0).astype(BF)
    last = pltpu.make_async_copy(tail, out.at[3 * MAIN :], sent.at[3])
    last.start()
    for copy in mains + [last]:
        copy.wait()


def pick_kernel(mine, near, off, high, low, to_near, to_off):
    even = is_even(mine)
    for i, (source, dy) in enumerate(((low, -1), (high, 1))):
        for side, target, out in ((-1, near, to_near), (1, off, to_off)):
            wanted = choose(even, side, dy, lambda o: head_cells(target, PARTNER, o))
            owners = choose(even, side, dy, lambda o: head_cells(source, OWN, o), True)
            out[i * WIDE : (i + 1) * WIDE] = nn(source[...], pick_table(wanted, owners)).astype(BF)
            digits = head_digits(choose(even, side, dy, lambda o: head_cells(source, PARTNER, o), True))
            cells = jnp.concatenate([d.astype(F32) for d in digits], axis=1)
            rot = choose(even, side, dy, lambda o: head_rots(source, o), True).astype(F32)
            row = iota((HEAD, PAIR), 0)
            head = jnp.where(row == 0, cells, jnp.where(row == 1, jnp.concatenate([rot, rot], axis=1), 0.0))
            out[i * WIDE + HEAD_AT : (i + 1) * WIDE] = head.astype(BF)


PHASES = {
    "here": ((0, 0),),
    "sides": ((1, 0), (-1, 0)),
    "middle": ((0, -1), (0, 1), (1, -1), (1, 1)),
    "end": ((-1, -1), (-1, 1)),
}


def phase_kernel(kind, *refs):
    sources = PHASES[kind]
    first, last = kind == "here", kind == "end"
    m = len(sources)
    mine = refs[0]
    even = is_even(mine)
    count = {"here": 1, "sides": 3, "middle": 4, "end": 2}[kind]
    arrays, refs = refs[:count], refs[count:]
    rot_ref, rot_tail, trans_main, trans_tail = refs[:4]
    refs = refs[4:]
    if first:
        self_main, self_tail = refs[:2]
        refs = refs[2:]
    else:
        acc_in = refs[0]
        refs = refs[1:]
    out, grouped, turned, places_to = refs[:4]
    sums = refs[4] if last else out

    def forwarded(s):
        side, dy = sources[s]
        return side and dy

    def other(s):
        side, dy = sources[s]
        if forwarded(s):
            return arrays[-1], (0 if dy < 0 else WIDE)
        return arrays[s if first else s + 1], 0

    def cell_pair(s, mine_what, their_what):
        array, start = other(s)
        ours = choose(even, *sources[s], lambda o: head_cells(mine, mine_what, o))
        if forwarded(s):
            return ours, head_cells(array, OWN, 0, start + HEAD_AT)
        return ours, choose(even, *sources[s], lambda o: head_cells(array, their_what, o), True)

    def rot_pair(s):
        array, start = other(s)
        ours = choose(even, *sources[s], lambda o: head_rots(mine, o))
        if forwarded(s):
            return ours, head_part(array, start + HEAD_AT, 1, 0).astype(jnp.int32)
        return ours, choose(even, *sources[s], lambda o: head_rots(array, o), True)

    if first:
        rows = nt(eye(CELLS), mine[...]).astype(BF)
        for lanes, part in zip(COLUMNS, apply_dense(rows, self_main, self_tail)):
            out[:, lanes] = part

    rots = []
    for s in range(m):
        rots.extend(rot_pair(s))
    places = positions(rots)

    for s in range(m):
        array, start = other(s)
        if forwarded(s):
            taken = array[start : start + WIDE]
        else:
            table = pick_table(*cell_pair(s, PARTNER, OWN))
            taken = nn(array[...], table).astype(BF)
        row_ids = iota((ROWS, SLOTS), 0)
        own_place, partner_place = places[2 * s], places[2 * s + 1]
        place = jnp.concatenate([where_one(row_ids == own_place), where_one(row_ids == partner_place)], axis=1)
        lanes = slice(s * GROUP, (s + 1) * GROUP)
        grouped[:, lanes, :] = nt(place, taken).astype(BF).reshape(NR, GROUP, WIDE)
        own_to, partner_to = cell_pair(s, OWN, PARTNER)
        to = jnp.concatenate([own_to, partner_to], axis=1) + 1
        digits = jnp.concatenate([to // BASE, to % BASE, jnp.zeros((6, PAIR), jnp.int32)], axis=0)
        back = nt(digits.astype(F32).astype(BF), place)
        goal = (back[0:1] * BASE + back[1:2]).astype(jnp.int32) - 1
        places_to[:, s * ROWS : (s + 1) * ROWS] = where_one(iota((CELLS, ROWS), 0) == goal)

    size = m * GROUP
    main_signs = side_signs(MAIN, 0)
    tail_signs = side_signs(TAIL, MAIN)

    def turn(r, source, target, dot):
        block = source[r]
        mains, tail = split_lanes(block)
        turned_main = dot(jnp.concatenate(mains, axis=0), rot_ref[r, :MAIN, :MAIN])
        turned_main = (turned_main.reshape(3 * m, GROUP, MAIN) * main_signs[None]).reshape(3 * size, MAIN)
        for c in range(3):
            target[r, :, c * MAIN : (c + 1) * MAIN] = turned_main[c * size : (c + 1) * size].astype(BF)
        target[r, :, 3 * MAIN :] = dot(tail, rot_tail[r]).astype(BF)

    for r in range(NR):
        turn(r, grouped, turned, nt)

    block = turned[...].reshape(NR * size, WIDE)
    for lanes, part in zip(COLUMNS, apply_dense(block, trans_main, trans_tail)):
        grouped[:, :, lanes] = part.astype(BF).reshape(NR, size, lanes.stop - lanes.start)

    for r in range(NR):
        turn(r, grouped, turned, nn)

    for lanes in COLUMNS:
        width = lanes.stop - lanes.start
        back = [turned[:, s * GROUP : (s + 1) * GROUP, lanes].reshape(ROWS, width) for s in range(m)]
        total = nn(places_to[...], jnp.concatenate(back, axis=0))
        sums[:, lanes] = total + (sums[:, lanes] if first else acc_in[:, lanes])
    if last:
        tail = sums[:, 3 * MAIN :].astype(BF)
        unit = eye(MAIN)
        for c in range(3):
            out[c, :MAIN, :] = nt(unit, sums[:, c * MAIN : (c + 1) * MAIN].astype(BF)).astype(BF)
            gather = where_one(iota((REST, TAIL), 1) == iota((REST, TAIL), 0) + c * REST)
            out[c, MAIN:, :] = nt(gather, tail).astype(BF)


def vmem_call(kernel, out_shape, scratch=(), limit=VMEM_LIMIT, cost=1000, **options):
    return pl.pallas_call(
        kernel,
        out_shape=out_shape,
        scratch_shapes=list(scratch),
        compiler_params=pltpu.CompilerParams(vmem_limit_bytes=limit),
        cost_estimate=pl.CostEstimate(flops=cost, bytes_accessed=1000, transcendentals=0),
        **options,
    )


def phase_call(kind):
    m, last = len(PHASES[kind]), kind == "end"
    if last:
        out = jax.ShapeDtypeStruct((3, K, CELLS), BF)
    else:
        out = jax.ShapeDtypeStruct((CELLS, WIDE), F32)
    scratch = [
        pltpu.VMEM((NR, m * GROUP, WIDE), BF),
        pltpu.VMEM((NR, m * GROUP, WIDE), BF),
        pltpu.VMEM((CELLS, m * ROWS), BF),
    ]
    if last:
        scratch.append(pltpu.VMEM((CELLS, WIDE), F32))
    cost = HERE_COST if kind == "here" else 1000
    return vmem_call(functools.partial(phase_kernel, kind), out, scratch, cost=cost)


def swap(block, first):
    count = lax.axis_size("gx")
    return lax.ppermute(block, "gx", [(i, (i + (first if i % 2 == 0 else -first)) % count) for i in range(count)])


def shift(block, axis, distance):
    count = lax.axis_size(axis)
    return lax.ppermute(block, axis, [((i - distance) % count, i) for i in range(count)])


def local(traction, self_operator, translation, rotations, own_cell, partner_cell, rot_index, block_count):
    here = traction.reshape(3, K, CELLS)
    slots = [a.reshape(9, 1, SLOTS) for a in (own_cell, partner_cell, rot_index)]
    there = pl.BlockSpec(memory_space=pl.ANY)
    mine = vmem_call(
        pack_kernel,
        jax.ShapeDtypeStruct((WIDE, CELLS), BF),
        [pltpu.SMEM((1, 9), jnp.int32)]
        + [pltpu.VMEM((9, 1, SLOTS), jnp.int32)] * 3
        + [pltpu.VMEM((3, K, CELLS), BF), pltpu.VMEM((TAIL, CELLS), BF)]
        + [pltpu.SemaphoreType.DMA((5,)), pltpu.SemaphoreType.DMA((4,))],
        limit=PACK_LIMIT,
        in_specs=[there] * 5,
        out_specs=there,
    )(block_count.reshape(1, 9), *slots, here)
    after = lax.optimization_barrier
    near, off = swap(mine, 1), swap(mine, -1)
    high, low = shift(mine, "gy", -1), shift(mine, "gy", 1)

    dense = [
        jax.ShapeDtypeStruct((3, MAIN, MAIN + TAIL), BF),
        jax.ShapeDtypeStruct((TAIL, WIDE), BF),
    ]
    rot_tail, *dense = vmem_call(
        prep_kernel, [jax.ShapeDtypeStruct((NR, TAIL, TAIL), BF)] + dense + dense
    )(rotations, translation, self_operator)
    weights = (rotations, rot_tail, *dense[:2])

    acc = phase_call("here")(mine, *weights, *dense[2:])
    acc = phase_call("sides")(mine, near, off, *weights, acc)
    acc, high, low = after((acc, high, low))
    picked = jax.ShapeDtypeStruct((2 * WIDE, PAIR), BF)
    to_near, to_off = vmem_call(pick_kernel, (picked, picked))(mine, near, off, high, low)
    far_near, far_off = swap(to_near, 1), swap(to_off, -1)
    acc = phase_call("middle")(mine, low, high, far_near, *weights, acc)
    velocity = phase_call("end")(mine, far_off, *weights, acc)
    return velocity.reshape(3, K, 1, 1, CELLS)


def solution(mesh):
    return jax.shard_map(
        local,
        mesh=mesh,
        in_specs=(
            P(None, None, "gx", "gy", None),
            P(),
            P(),
            P(),
            P("gx", "gy", None, None),
            P("gx", "gy", None, None),
            P("gx", "gy", None, None, None),
            P("gx", "gy", None),
        ),
        out_specs=P(None, None, "gx", "gy", None),
        check_vma=False,
    )
```

```python
import functools

import jax
import jax.numpy as jnp
from jax import lax
from jax.experimental import pallas as pl
from jax.experimental.pallas import tpu as pltpu
from jax.sharding import PartitionSpec as P

BF = jnp.bfloat16
F32 = jnp.float32

K = 289
MAIN = 256
REST = K - MAIN
TAIL = 128
WIDE = 3 * MAIN + TAIL
CELLS = 512
SLOTS = 128
NR = 16
CAP = 16
PAIR = 2 * SLOTS
GROUP = 2 * CAP
ROWS = NR * GROUP
LONG = 880
SLAB = 16
SLAB_AT = LONG - SLAB
HEAD = 13
ABOVE = SLAB - HEAD
BASE = 32
OWN, PARTNER = 0, 2
ROT = 9
ODD = 12
COLUMNS = (slice(0, 256), slice(256, 512), slice(512, 768), slice(768, 896))
VMEM_LIMIT = 28 * 1024 * 1024
HERE_COST = 30_000_000_000
PACK_LIMIT = 62 * 1024 * 1024


def nt(a, b):
    return lax.dot_general(a, b, (((1,), (1,)), ((), ())), preferred_element_type=F32)


def nn(a, b):
    return jnp.dot(a, b, preferred_element_type=F32)


def iota(shape, dim):
    return lax.broadcasted_iota(jnp.int32, shape, dim)


def where_one(condition):
    return jnp.where(condition, 1.0, 0.0).astype(BF)


def eye(size):
    return where_one(iota((size, size), 0) == iota((size, size), 1))


def spread(c):
    return where_one(iota((TAIL, REST), 0) == iota((TAIL, REST), 1) + c * REST)


def offset_of(dx, dy):
    return (dx + 1) * 3 + dy + 1


def offsets(side, dy):
    return offset_of(side, dy), offset_of(-side, dy)


def choose(even, side, dy, read, theirs=False):
    first, second = [8 - o if theirs else o for o in offsets(side, dy)]
    return read(first) if first == second else jnp.where(even, read(first), read(second))


def parity_lanes(width, start):
    k = iota((1, width), 1) + start
    degree = jnp.zeros((1, width), jnp.int32)
    for level in range(1, 17):
        degree = degree + jnp.where(k >= level * level, 1, 0)
    return 1.0 - 2.0 * (degree % 2).astype(F32)


def side_signs(width, start):
    signs = jnp.broadcast_to(parity_lanes(width, start), (GROUP, width))
    return jnp.where(iota((GROUP, width), 0) >= CAP, signs, 1.0)


def pick_table(own_side, partner_side):
    cells = iota((CELLS, SLOTS), 0)
    return jnp.concatenate([where_one(cells == own_side), where_one(cells == partner_side)], axis=1)


def positions(rots):
    marks = [where_one(iota((NR, SLOTS), 0) == rot) for rot in rots]
    earlier = where_one(iota((SLOTS, SLOTS), 0) < iota((SLOTS, SLOTS), 1))
    ranks = nn(jnp.concatenate(marks, axis=0), earlier)
    places = []
    for j, mark in enumerate(marks):
        base = (iota((NR, SLOTS), 0) * GROUP + (j % 2) * CAP + 1).astype(F32)
        values = mark.astype(F32) * (ranks[j * NR : (j + 1) * NR] + base)
        places.append(jnp.sum(values, axis=0, keepdims=True).astype(jnp.int32) - 1)
    return places


def apply_dense(block, main_ref, tail_ref):
    tail = block[:, 3 * MAIN :]
    outs = [
        nt(jnp.concatenate([block[:, c * MAIN : (c + 1) * MAIN], tail], axis=1), main_ref[c]) for c in range(3)
    ]
    return outs + [nt(block, tail_ref[...])]


def split_lanes(block):
    return [block[:, c * MAIN : (c + 1) * MAIN] for c in range(3)], block[:, 3 * MAIN :]


def prep_kernel(rot_ref, trans_ref, self_ref, rot_tail, *pieces):
    fold = where_one((iota((TAIL, REST), 0) % REST == iota((TAIL, REST), 1)) & (iota((TAIL, REST), 0) < 3 * REST))
    same = (iota((TAIL, TAIL), 0) // REST) == (iota((TAIL, TAIL), 1) // REST)

    def tail_block(block):
        return jnp.where(same, nt(nn(fold, block).astype(BF), fold), 0.0).astype(BF)

    rot_tail[...] = jnp.zeros(rot_tail.shape, BF)
    for r in range(NR):
        place = slice(r % 2 * TAIL, (r % 2 + 1) * TAIL)
        rot_tail[r // 2, place, place] = tail_block(rot_ref[r, MAIN:, MAIN:])
    for source, (main, tail) in ((trans_ref, pieces[:2]), (self_ref, pieces[2:])):
        for c in range(3):
            main[c, :, :MAIN] = source[:MAIN, :MAIN]
            main[c, :, MAIN:] = nt(source[:MAIN, MAIN:], spread(c)).astype(BF)
            tail[:, c * MAIN : (c + 1) * MAIN] = nn(spread(c), source[MAIN:, :MAIN]).astype(BF)
        tail[:, 3 * MAIN :] = tail_block(source[MAIN:, MAIN:])


def head_part(ref, at, row, block):
    lanes = slice(block * SLOTS, (block + 1) * SLOTS)
    return ref[at : at + SLAB, lanes].astype(F32)[row + ABOVE : row + ABOVE + 1]


def head_cells(ref, what, row, at=SLAB_AT):
    return (head_part(ref, at, row, what) * BASE + head_part(ref, at, row, what + 1)).astype(jnp.int32)


def head_rots(ref, o):
    return head_part(ref, SLAB_AT, ROT + o // 4, o % 4).astype(jnp.int32)


def is_even(mine):
    return head_part(mine, SLAB_AT, ODD, 0) < 0.5


def head_digits(index):
    high = index // BASE
    return high.astype(F32).astype(BF), (index - high * BASE).astype(F32).astype(BF)


def pack_kernel(count_ref, own_ref, partner_ref, rot_ref, here_ref, out, *scratch):
    held, tail, arrived, sent = scratch[:5], scratch[5], scratch[6], scratch[7]
    count, own, partner, rot, here = held
    bodies = [pltpu.make_async_copy(here_ref.at[c], here.at[c], arrived.at[c]) for c in range(3)]
    small = [
        pltpu.make_async_copy(src, dst, arrived.at[3 + i])
        for i, (src, dst) in enumerate(zip((count_ref, own_ref, partner_ref, rot_ref), held))
    ]
    for copy in bodies + small:
        copy.start()
    sends = [
        pltpu.make_async_copy(here.at[c, :MAIN], out.at[c * MAIN : (c + 1) * MAIN], sent.at[c]) for c in range(3)
    ]
    for body, send in zip(bodies, sends):
        body.wait()
        send.start()
    for copy in small:
        copy.wait()
    rest = nn(spread(0), here[0, MAIN:]) + nn(spread(1), here[1, MAIN:]) + nn(spread(2), here[2, MAIN:])
    cells = [jnp.concatenate([ref[o] for o in range(9)], axis=0) for ref in (own, partner)]
    digits = jnp.concatenate([d.astype(F32) for index in cells for d in head_digits(index)], axis=1)
    slot = iota((1, SLOTS), 1)
    live = [jnp.where(slot < count[0, o], rot[o], NR).astype(F32) for o in range(9)]
    live.extend([jnp.zeros((1, SLOTS), F32)] * 3)
    rots = [jnp.concatenate(live[4 * i : 4 * i + 4], axis=1) for i in range(3)]
    odd = lax.rem(lax.axis_index("gx"), 2)
    flags = jnp.where(iota((1, CELLS), 0) + odd > 0, 1.0, 0.0)
    head = jnp.concatenate([jnp.zeros((3 * REST, CELLS), F32), digits, *rots, flags], axis=0)
    tail[...] = (rest[: LONG - 3 * MAIN] + head).astype(BF)
    last = pltpu.make_async_copy(tail, out.at[3 * MAIN :], sent.at[3])
    last.start()
    for copy in sends + [last]:
        copy.wait()


def pick_kernel(mine, near, off, high, low, to_near, to_off):
    even = is_even(mine)
    for i, (source, dy) in enumerate(((low, -1), (high, 1))):
        for side, target, out in ((-1, near, to_near), (1, off, to_off)):
            wanted = choose(even, side, dy, lambda o: head_cells(target, PARTNER, o))
            owners = choose(even, side, dy, lambda o: head_cells(source, OWN, o), True)
            picked = nn(source[...], pick_table(wanted, owners))
            out[i * LONG : i * LONG + SLAB_AT] = picked[:SLAB_AT].astype(BF)
            digits = head_digits(choose(even, side, dy, lambda o: head_cells(source, PARTNER, o), True))
            cells = jnp.concatenate([d.astype(F32) for d in digits], axis=1)
            rot = choose(even, side, dy, lambda o: head_rots(source, o), True).astype(F32)
            row = iota((SLAB, PAIR), 0) - ABOVE
            head = jnp.where(row == 0, cells, jnp.where(row == 1, jnp.concatenate([rot, rot], axis=1), 0.0))
            slab = jnp.where(row < 0, picked[SLAB_AT:], head)
            out[i * LONG + SLAB_AT : (i + 1) * LONG] = slab.astype(BF)


PHASES = {
    "here": ((0, 0),),
    "sides": ((1, 0), (-1, 0)),
    "middle": ((0, -1), (0, 1), (1, -1), (1, 1)),
    "end": ((-1, -1), (-1, 1)),
}


def phase_kernel(kind, *refs):
    sources = PHASES[kind]
    first, last = kind == "here", kind == "end"
    m = len(sources)
    mine = refs[0]
    even = is_even(mine)
    count = {"here": 1, "sides": 3, "middle": 4, "end": 2}[kind]
    arrays, refs = refs[:count], refs[count:]
    rot_ref, rot_tail, trans_main, trans_tail = refs[:4]
    refs = refs[4:]
    if first:
        self_main, self_tail = refs[:2]
        refs = refs[2:]
    else:
        acc_in = refs[0]
        refs = refs[1:]
    out, grouped, turned, places_to = refs[:4]
    sums = refs[4] if last else out

    def forwarded(s):
        side, dy = sources[s]
        return side and dy

    def other(s):
        side, dy = sources[s]
        if forwarded(s):
            return arrays[-1], (0 if dy < 0 else LONG)
        return arrays[s if first else s + 1], 0

    def cell_pair(s, mine_what, their_what):
        array, start = other(s)
        ours = choose(even, *sources[s], lambda o: head_cells(mine, mine_what, o))
        if forwarded(s):
            return ours, head_cells(array, OWN, 0, start + SLAB_AT)
        return ours, choose(even, *sources[s], lambda o: head_cells(array, their_what, o), True)

    def rot_pair(s):
        array, start = other(s)
        ours = choose(even, *sources[s], lambda o: head_rots(mine, o))
        if forwarded(s):
            return ours, head_part(array, start + SLAB_AT, 1, 0).astype(jnp.int32)
        return ours, choose(even, *sources[s], lambda o: head_rots(array, o), True)

    if first:
        whole = jnp.concatenate([mine[...], jnp.zeros((WIDE - LONG, CELLS), BF)], axis=0)
        rows = nt(eye(CELLS), whole).astype(BF)
        for lanes, part in zip(COLUMNS, apply_dense(rows, self_main, self_tail)):
            out[:, lanes] = part

    rots = []
    for s in range(m):
        rots.extend(rot_pair(s))
    places = positions(rots)

    for s in range(m):
        array, start = other(s)
        if forwarded(s):
            taken = array[start : start + LONG]
        else:
            table = pick_table(*cell_pair(s, PARTNER, OWN))
            taken = nn(array[...], table).astype(BF)
        row_ids = iota((ROWS, SLOTS), 0)
        own_place, partner_place = places[2 * s], places[2 * s + 1]
        place = jnp.concatenate([where_one(row_ids == own_place), where_one(row_ids == partner_place)], axis=1)
        lanes = slice(s * GROUP, (s + 1) * GROUP)
        taken = jnp.concatenate([taken, jnp.zeros((WIDE - LONG, PAIR), BF)], axis=0)
        grouped[:, lanes, :] = nt(place, taken).astype(BF).reshape(NR, GROUP, WIDE)
        own_to, partner_to = cell_pair(s, OWN, PARTNER)
        to = jnp.concatenate([own_to, partner_to], axis=1) + 1
        digits = jnp.concatenate([to // BASE, to % BASE, jnp.zeros((6, PAIR), jnp.int32)], axis=0)
        back = nt(digits.astype(F32).astype(BF), place)
        goal = (back[0:1] * BASE + back[1:2]).astype(jnp.int32) - 1
        places_to[:, s * ROWS : (s + 1) * ROWS] = where_one(iota((CELLS, ROWS), 0) == goal)

    size = m * GROUP
    main_signs = side_signs(MAIN, 0)

    def turn(pair, source, target, dot):
        tails = []
        for r in (2 * pair, 2 * pair + 1):
            mains, tail = split_lanes(source[r])
            tails.append(tail)
            turned_main = dot(jnp.concatenate(mains, axis=0), rot_ref[r, :MAIN, :MAIN])
            turned_main = (turned_main.reshape(3 * m, GROUP, MAIN) * main_signs[None]).reshape(3 * size, MAIN)
            for c in range(3):
                target[r, :, c * MAIN : (c + 1) * MAIN] = turned_main[c * size : (c + 1) * size].astype(BF)
        both = dot(jnp.concatenate(tails, axis=1), rot_tail[pair]).astype(BF)
        target[2 * pair, :, 3 * MAIN :] = both[:, :TAIL]
        target[2 * pair + 1, :, 3 * MAIN :] = both[:, TAIL:]

    for pair in range(NR // 2):
        turn(pair, grouped, turned, nt)

    block = turned[...].reshape(NR * size, WIDE)
    for lanes, part in zip(COLUMNS, apply_dense(block, trans_main, trans_tail)):
        grouped[:, :, lanes] = part.astype(BF).reshape(NR, size, lanes.stop - lanes.start)

    for pair in range(NR // 2):
        turn(pair, grouped, turned, nn)

    for lanes in COLUMNS:
        width = lanes.stop - lanes.start
        back = [turned[:, s * GROUP : (s + 1) * GROUP, lanes].reshape(ROWS, width) for s in range(m)]
        total = nn(places_to[...], jnp.concatenate(back, axis=0))
        sums[:, lanes] = total + (sums[:, lanes] if first else acc_in[:, lanes])
    if last:
        tail = sums[:, 3 * MAIN :].astype(BF).T
        for c in range(3):
            out[c, :MAIN, :] = sums[:, c * MAIN : (c + 1) * MAIN].astype(BF).T
            gather = where_one(iota((REST, TAIL), 1) == iota((REST, TAIL), 0) + c * REST)
            out[c, MAIN:, :] = nn(gather, tail).astype(BF)


def vmem_call(kernel, out_shape, scratch=(), limit=VMEM_LIMIT, cost=1000, **options):
    return pl.pallas_call(
        kernel,
        out_shape=out_shape,
        scratch_shapes=list(scratch),
        compiler_params=pltpu.CompilerParams(vmem_limit_bytes=limit),
        cost_estimate=pl.CostEstimate(flops=cost, bytes_accessed=1000, transcendentals=0),
        **options,
    )


def phase_call(kind):
    m, last = len(PHASES[kind]), kind == "end"
    if last:
        out = jax.ShapeDtypeStruct((3, K, CELLS), BF)
    else:
        out = jax.ShapeDtypeStruct((CELLS, WIDE), F32)
    scratch = [
        pltpu.VMEM((NR, m * GROUP, WIDE), BF),
        pltpu.VMEM((NR, m * GROUP, WIDE), BF),
        pltpu.VMEM((CELLS, m * ROWS), BF),
    ]
    if last:
        scratch.append(pltpu.VMEM((CELLS, WIDE), F32))
    cost = HERE_COST if kind == "here" else 1000
    return vmem_call(functools.partial(phase_kernel, kind), out, scratch, cost=cost)


def swap(block, first):
    count = lax.axis_size("gx")
    return lax.ppermute(block, "gx", [(i, (i + (first if i % 2 == 0 else -first)) % count) for i in range(count)])


def shift(block, axis, distance):
    count = lax.axis_size(axis)
    return lax.ppermute(block, axis, [((i - distance) % count, i) for i in range(count)])


def local(traction, self_operator, translation, rotations, own_cell, partner_cell, rot_index, block_count):
    here = traction.reshape(3, K, CELLS)
    slots = [a.reshape(9, 1, SLOTS) for a in (own_cell, partner_cell, rot_index)]
    there = pl.BlockSpec(memory_space=pl.ANY)
    mine = vmem_call(
        pack_kernel,
        jax.ShapeDtypeStruct((LONG, CELLS), BF),
        [pltpu.SMEM((1, 9), jnp.int32)]
        + [pltpu.VMEM((9, 1, SLOTS), jnp.int32)] * 3
        + [pltpu.VMEM((3, K, CELLS), BF), pltpu.VMEM((LONG - 3 * MAIN, CELLS), BF)]
        + [pltpu.SemaphoreType.DMA((7,)), pltpu.SemaphoreType.DMA((4,))],
        limit=PACK_LIMIT,
        in_specs=[there] * 5,
        out_specs=there,
    )(block_count.reshape(1, 9), *slots, here)
    after = lax.optimization_barrier
    near, off = swap(mine, 1), swap(mine, -1)
    high, low = shift(mine, "gy", -1), shift(mine, "gy", 1)

    dense = [
        jax.ShapeDtypeStruct((3, MAIN, MAIN + TAIL), BF),
        jax.ShapeDtypeStruct((TAIL, WIDE), BF),
    ]
    rot_tail, *dense = vmem_call(
        prep_kernel, [jax.ShapeDtypeStruct((NR // 2, 2 * TAIL, 2 * TAIL), BF)] + dense + dense
    )(rotations, translation, self_operator)
    weights = (rotations, rot_tail, *dense[:2])

    acc = phase_call("here")(mine, *weights, *dense[2:])
    acc = phase_call("sides")(mine, near, off, *weights, acc)
    acc, high, low = after((acc, high, low))
    picked = jax.ShapeDtypeStruct((2 * LONG, PAIR), BF)
    to_near, to_off = vmem_call(pick_kernel, (picked, picked))(mine, near, off, high, low)
    far_near, far_off = swap(to_near, 1), swap(to_off, -1)
    acc = phase_call("middle")(mine, low, high, far_near, *weights, acc)
    velocity = phase_call("end")(mine, far_off, *weights, acc)
    return velocity.reshape(3, K, 1, 1, CELLS)


def solution(mesh):
    return jax.shard_map(
        local,
        mesh=mesh,
        in_specs=(
            P(None, None, "gx", "gy", None),
            P(),
            P(),
            P(),
            P("gx", "gy", None, None),
            P("gx", "gy", None, None),
            P("gx", "gy", None, None, None),
            P("gx", "gy", None),
        ),
        out_specs=P(None, None, "gx", "gy", None),
        check_vma=False,
    )
```

```python
import functools

import jax
import jax.numpy as jnp
from jax import lax
from jax.experimental import pallas as pl
from jax.experimental.pallas import tpu as pltpu
from jax.sharding import PartitionSpec as P

BF = jnp.bfloat16
F32 = jnp.float32

K = 289
MAIN = 256
REST = K - MAIN
TAIL = 128
WIDE = 3 * MAIN + TAIL
CELLS = 512
SLOTS = 128
NR = 16
CAP = 16
PAIR = 2 * SLOTS
GROUP = 2 * CAP
ROWS = NR * GROUP
LONG = 880
SLAB = 16
SLAB_AT = LONG - SLAB
HEAD = 13
ABOVE = SLAB - HEAD
BASE = 32
OWN, PARTNER = 0, 2
CODE = 9
DEAD = NR * CAP
ODD = 12
COLUMNS = (slice(0, 256), slice(256, 512), slice(512, 768), slice(768, 896))
VMEM_LIMIT = 28 * 1024 * 1024
HERE_COST = 30_000_000_000
PACK_LIMIT = 62 * 1024 * 1024


def nt(a, b):
    return lax.dot_general(a, b, (((1,), (1,)), ((), ())), preferred_element_type=F32)


def nn(a, b):
    return jnp.dot(a, b, preferred_element_type=F32)


def iota(shape, dim):
    return lax.broadcasted_iota(jnp.int32, shape, dim)


def where_one(condition):
    return jnp.where(condition, 1.0, 0.0).astype(BF)


def eye(size):
    return where_one(iota((size, size), 0) == iota((size, size), 1))


def spread(c):
    return where_one(iota((TAIL, REST), 0) == iota((TAIL, REST), 1) + c * REST)


def offset_of(dx, dy):
    return (dx + 1) * 3 + dy + 1


def offsets(side, dy):
    return offset_of(side, dy), offset_of(-side, dy)


def choose(even, side, dy, read, theirs=False):
    first, second = [8 - o if theirs else o for o in offsets(side, dy)]
    return read(first) if first == second else jnp.where(even, read(first), read(second))


def parity_lanes(width, start):
    k = iota((1, width), 1) + start
    degree = jnp.zeros((1, width), jnp.int32)
    for level in range(1, 17):
        degree = degree + jnp.where(k >= level * level, 1, 0)
    return 1.0 - 2.0 * (degree % 2).astype(F32)


def side_signs(width, start):
    signs = jnp.broadcast_to(parity_lanes(width, start), (GROUP, width))
    return jnp.where(iota((GROUP, width), 0) >= CAP, signs, 1.0)


def pick_table(own_side, partner_side):
    cells = iota((CELLS, SLOTS), 0)
    return jnp.concatenate([where_one(cells == own_side), where_one(cells == partner_side)], axis=1)


def ranks_of(rots):
    marks = [where_one(iota((NR, SLOTS), 0) == rot) for rot in rots]
    earlier = where_one(iota((SLOTS, SLOTS), 0) < iota((SLOTS, SLOTS), 1))
    counts = nn(jnp.concatenate(marks, axis=0), earlier)
    return [
        jnp.sum(mark.astype(F32) * counts[o * NR : (o + 1) * NR], axis=0, keepdims=True).astype(jnp.int32)
        for o, mark in enumerate(marks)
    ]


def place_rows(codes):
    rows = [code + code // CAP * CAP + side * CAP for side, code in enumerate(codes)]
    return [jnp.where(code >= DEAD, -1, row) for code, row in zip(codes, rows)]


def apply_dense(block, main_ref, tail_ref):
    tail = block[:, 3 * MAIN :]
    outs = [
        nt(jnp.concatenate([block[:, c * MAIN : (c + 1) * MAIN], tail], axis=1), main_ref[c]) for c in range(3)
    ]
    return outs + [nt(block, tail_ref[...])]


def split_lanes(block):
    return [block[:, c * MAIN : (c + 1) * MAIN] for c in range(3)], block[:, 3 * MAIN :]


def prep_kernel(rot_ref, trans_ref, self_ref, rot_tail, *pieces):
    fold = where_one((iota((TAIL, REST), 0) % REST == iota((TAIL, REST), 1)) & (iota((TAIL, REST), 0) < 3 * REST))
    same = (iota((TAIL, TAIL), 0) // REST) == (iota((TAIL, TAIL), 1) // REST)

    def tail_block(block):
        return jnp.where(same, nt(nn(fold, block).astype(BF), fold), 0.0).astype(BF)

    rot_tail[...] = jnp.zeros(rot_tail.shape, BF)
    for r in range(NR):
        place = slice(r % 2 * TAIL, (r % 2 + 1) * TAIL)
        rot_tail[r // 2, place, place] = tail_block(rot_ref[r, MAIN:, MAIN:])
    for source, (main, tail) in ((trans_ref, pieces[:2]), (self_ref, pieces[2:])):
        for c in range(3):
            main[c, :, :MAIN] = source[:MAIN, :MAIN]
            main[c, :, MAIN:] = nt(source[:MAIN, MAIN:], spread(c)).astype(BF)
            tail[:, c * MAIN : (c + 1) * MAIN] = nn(spread(c), source[MAIN:, :MAIN]).astype(BF)
        tail[:, 3 * MAIN :] = tail_block(source[MAIN:, MAIN:])


def head_part(ref, at, row, block):
    lanes = slice(block * SLOTS, (block + 1) * SLOTS)
    return ref[at : at + SLAB, lanes].astype(F32)[row + ABOVE : row + ABOVE + 1]


def head_cells(ref, what, row, at=SLAB_AT):
    return (head_part(ref, at, row, what) * BASE + head_part(ref, at, row, what + 1)).astype(jnp.int32)


def head_codes(ref, o):
    return head_part(ref, SLAB_AT, CODE + o // 4, o % 4).astype(jnp.int32)


def is_even(mine):
    return head_part(mine, SLAB_AT, ODD, 0) < 0.5


def head_digits(index):
    high = index // BASE
    return high.astype(F32).astype(BF), (index - high * BASE).astype(F32).astype(BF)


def pack_kernel(count_ref, own_ref, partner_ref, rot_ref, here_ref, out, *scratch):
    held, tail, arrived, sent = scratch[:5], scratch[5], scratch[6], scratch[7]
    count, own, partner, rot, here = held
    small = [
        pltpu.make_async_copy(src, dst, arrived.at[3 + i])
        for i, (src, dst) in enumerate(zip((count_ref, own_ref, partner_ref, rot_ref), held))
    ]
    bodies = [pltpu.make_async_copy(here_ref.at[c], here.at[c], arrived.at[c]) for c in range(3)]
    for copy in small + bodies:
        copy.start()
    for copy in small:
        copy.wait()
    slot = iota((1, SLOTS), 1)
    live = [slot < count[0, o] for o in range(9)]
    ranks = ranks_of([rot[o] for o in range(9)])
    codes = [jnp.where(live[o], rot[o] * CAP + ranks[o], DEAD).astype(F32) for o in range(9)]
    codes.extend([jnp.zeros((1, SLOTS), F32)] * 3)
    code_rows = [jnp.concatenate(codes[4 * i : 4 * i + 4], axis=1) for i in range(3)]
    cells = [jnp.concatenate([ref[o] for o in range(9)], axis=0) for ref in (own, partner)]
    digits = jnp.concatenate([d.astype(F32) for index in cells for d in head_digits(index)], axis=1)
    odd = lax.rem(lax.axis_index("gx"), 2)
    flags = jnp.where(iota((1, CELLS), 0) + odd > 0, 1.0, 0.0)
    head = jnp.concatenate([jnp.zeros((3 * REST, CELLS), F32), digits, *code_rows, flags], axis=0)
    sends = [
        pltpu.make_async_copy(here.at[c, :MAIN], out.at[c * MAIN : (c + 1) * MAIN], sent.at[c]) for c in range(3)
    ]
    for body, send in zip(bodies, sends):
        body.wait()
        send.start()
    rest = nn(spread(0), here[0, MAIN:]) + nn(spread(1), here[1, MAIN:]) + nn(spread(2), here[2, MAIN:])
    tail[...] = (rest[: LONG - 3 * MAIN] + head).astype(BF)
    last = pltpu.make_async_copy(tail, out.at[3 * MAIN :], sent.at[3])
    last.start()
    for copy in sends + [last]:
        copy.wait()


def pick_kernel(mine, near, off, high, low, to_near, to_off):
    even = is_even(mine)
    for i, (source, dy) in enumerate(((low, -1), (high, 1))):
        for side, target, out in ((-1, near, to_near), (1, off, to_off)):
            wanted = choose(even, side, dy, lambda o: head_cells(target, PARTNER, o))
            owners = choose(even, side, dy, lambda o: head_cells(source, OWN, o), True)
            picked = nn(source[...], pick_table(wanted, owners))
            out[i * LONG : i * LONG + SLAB_AT] = picked[:SLAB_AT].astype(BF)
            digits = head_digits(choose(even, side, dy, lambda o: head_cells(source, PARTNER, o), True))
            cells = jnp.concatenate([d.astype(F32) for d in digits], axis=1)
            rot = choose(even, side, dy, lambda o: head_codes(source, o), True).astype(F32)
            row = iota((SLAB, PAIR), 0) - ABOVE
            head = jnp.where(row == 0, cells, jnp.where(row == 1, jnp.concatenate([rot, rot], axis=1), 0.0))
            slab = jnp.where(row < 0, picked[SLAB_AT:], head)
            out[i * LONG + SLAB_AT : (i + 1) * LONG] = slab.astype(BF)


PHASES = {
    "here": ((0, 0),),
    "sides": ((1, 0), (-1, 0)),
    "middle": ((0, -1), (0, 1), (1, -1), (1, 1)),
    "end": ((-1, -1), (-1, 1)),
}


def phase_kernel(kind, *refs):
    sources = PHASES[kind]
    first, last = kind == "here", kind == "end"
    m = len(sources)
    mine = refs[0]
    even = is_even(mine)
    count = {"here": 1, "sides": 3, "middle": 4, "end": 2}[kind]
    arrays, refs = refs[:count], refs[count:]
    rot_ref, rot_tail, trans_main, trans_tail = refs[:4]
    refs = refs[4:]
    if first:
        self_main, self_tail = refs[:2]
        refs = refs[2:]
    else:
        acc_in = refs[0]
        refs = refs[1:]
    out, grouped, turned, places_to = refs

    def forwarded(s):
        side, dy = sources[s]
        return side and dy

    def other(s):
        side, dy = sources[s]
        if forwarded(s):
            return arrays[-1], (0 if dy < 0 else LONG)
        return arrays[s if first else s + 1], 0

    def cell_pair(s, mine_what, their_what):
        array, start = other(s)
        ours = choose(even, *sources[s], lambda o: head_cells(mine, mine_what, o))
        if forwarded(s):
            return ours, head_cells(array, OWN, 0, start + SLAB_AT)
        return ours, choose(even, *sources[s], lambda o: head_cells(array, their_what, o), True)

    def code_pair(s):
        array, start = other(s)
        ours = choose(even, *sources[s], lambda o: head_codes(mine, o))
        if forwarded(s):
            return ours, head_part(array, start + SLAB_AT, 1, 0).astype(jnp.int32)
        return ours, choose(even, *sources[s], lambda o: head_codes(array, o), True)

    if first:
        whole = jnp.concatenate([mine[...], jnp.zeros((WIDE - LONG, CELLS), BF)], axis=0)
        rows = nt(eye(CELLS), whole).astype(BF)
        for lanes, part in zip(COLUMNS, apply_dense(rows, self_main, self_tail)):
            out[:, lanes] = part

    for s in range(m):
        array, start = other(s)
        if forwarded(s):
            taken = array[start : start + LONG]
        else:
            table = pick_table(*cell_pair(s, PARTNER, OWN))
            taken = nn(array[...], table).astype(BF)
        row_ids = iota((ROWS, SLOTS), 0)
        own_place, partner_place = place_rows(code_pair(s))
        place = jnp.concatenate([where_one(row_ids == own_place), where_one(row_ids == partner_place)], axis=1)
        lanes = slice(s * GROUP, (s + 1) * GROUP)
        taken = jnp.concatenate([taken, jnp.zeros((WIDE - LONG, PAIR), BF)], axis=0)
        grouped[:, lanes, :] = nt(place, taken).astype(BF).reshape(NR, GROUP, WIDE)
        own_to, partner_to = cell_pair(s, OWN, PARTNER)
        to = jnp.concatenate([own_to, partner_to], axis=1) + 1
        digits = jnp.concatenate([to // BASE, to % BASE, jnp.zeros((6, PAIR), jnp.int32)], axis=0)
        back = nt(digits.astype(F32).astype(BF), place)
        goal = (back[0:1] * BASE + back[1:2]).astype(jnp.int32) - 1
        places_to[:, s * ROWS : (s + 1) * ROWS] = where_one(iota((CELLS, ROWS), 0) == goal)

    size = m * GROUP
    main_signs = side_signs(MAIN, 0)

    def turn(pair, source, target, dot):
        tails = []
        for r in (2 * pair, 2 * pair + 1):
            mains, tail = split_lanes(source[r])
            tails.append(tail)
            turned_main = dot(jnp.concatenate(mains, axis=0), rot_ref[r, :MAIN, :MAIN])
            turned_main = (turned_main.reshape(3 * m, GROUP, MAIN) * main_signs[None]).reshape(3 * size, MAIN)
            for c in range(3):
                target[r, :, c * MAIN : (c + 1) * MAIN] = turned_main[c * size : (c + 1) * size].astype(BF)
        both = dot(jnp.concatenate(tails, axis=1), rot_tail[pair]).astype(BF)
        target[2 * pair, :, 3 * MAIN :] = both[:, :TAIL]
        target[2 * pair + 1, :, 3 * MAIN :] = both[:, TAIL:]

    for pair in range(NR // 2):
        turn(pair, grouped, turned, nt)

    block = turned[...].reshape(NR * size, WIDE)
    for lanes, part in zip(COLUMNS, apply_dense(block, trans_main, trans_tail)):
        grouped[:, :, lanes] = part.astype(BF).reshape(NR, size, lanes.stop - lanes.start)

    for pair in range(NR // 2):
        turn(pair, grouped, turned, nn)

    for c, lanes in enumerate(COLUMNS):
        width = lanes.stop - lanes.start
        back = [turned[:, s * GROUP : (s + 1) * GROUP, lanes].reshape(ROWS, width) for s in range(m)]
        total = nn(places_to[...], jnp.concatenate(back, axis=0))
        total = total + (out[:, lanes] if first else acc_in[:, lanes])
        if not last:
            out[:, lanes] = total
        elif c < 3:
            out[c, :MAIN, :] = total.astype(BF).T
        else:
            tail = total.astype(BF).T
            for part in range(3):
                gather = where_one(iota((REST, TAIL), 1) == iota((REST, TAIL), 0) + part * REST)
                out[part, MAIN:, :] = nn(gather, tail).astype(BF)


def vmem_call(kernel, out_shape, scratch=(), limit=VMEM_LIMIT, cost=1000, **options):
    return pl.pallas_call(
        kernel,
        out_shape=out_shape,
        scratch_shapes=list(scratch),
        compiler_params=pltpu.CompilerParams(vmem_limit_bytes=limit),
        cost_estimate=pl.CostEstimate(flops=cost, bytes_accessed=1000, transcendentals=0),
        **options,
    )


def phase_call(kind):
    m, last = len(PHASES[kind]), kind == "end"
    if last:
        out = jax.ShapeDtypeStruct((3, K, CELLS), BF)
    else:
        out = jax.ShapeDtypeStruct((CELLS, WIDE), F32)
    scratch = [
        pltpu.VMEM((NR, m * GROUP, WIDE), BF),
        pltpu.VMEM((NR, m * GROUP, WIDE), BF),
        pltpu.VMEM((CELLS, m * ROWS), BF),
    ]
    cost = HERE_COST if kind == "here" else 1000
    return vmem_call(functools.partial(phase_kernel, kind), out, scratch, cost=cost)


def swap(block, first):
    count = lax.axis_size("gx")
    return lax.ppermute(block, "gx", [(i, (i + (first if i % 2 == 0 else -first)) % count) for i in range(count)])


def shift(block, axis, distance):
    count = lax.axis_size(axis)
    return lax.ppermute(block, axis, [((i - distance) % count, i) for i in range(count)])


def local(traction, self_operator, translation, rotations, own_cell, partner_cell, rot_index, block_count):
    here = traction.reshape(3, K, CELLS)
    slots = [a.reshape(9, 1, SLOTS) for a in (own_cell, partner_cell, rot_index)]
    there = pl.BlockSpec(memory_space=pl.ANY)
    mine = vmem_call(
        pack_kernel,
        jax.ShapeDtypeStruct((LONG, CELLS), BF),
        [pltpu.SMEM((1, 9), jnp.int32)]
        + [pltpu.VMEM((9, 1, SLOTS), jnp.int32)] * 3
        + [pltpu.VMEM((3, K, CELLS), BF), pltpu.VMEM((LONG - 3 * MAIN, CELLS), BF)]
        + [pltpu.SemaphoreType.DMA((7,)), pltpu.SemaphoreType.DMA((4,))],
        limit=PACK_LIMIT,
        in_specs=[there] * 5,
        out_specs=there,
    )(block_count.reshape(1, 9), *slots, here)
    after = lax.optimization_barrier
    near, off = swap(mine, 1), swap(mine, -1)
    high, low = shift(mine, "gy", -1), shift(mine, "gy", 1)

    dense = [
        jax.ShapeDtypeStruct((3, MAIN, MAIN + TAIL), BF),
        jax.ShapeDtypeStruct((TAIL, WIDE), BF),
    ]
    rot_tail, *dense = vmem_call(
        prep_kernel, [jax.ShapeDtypeStruct((NR // 2, 2 * TAIL, 2 * TAIL), BF)] + dense + dense
    )(rotations, translation, self_operator)
    weights = (rotations, rot_tail, *dense[:2])

    acc = phase_call("here")(mine, *weights, *dense[2:])
    acc = phase_call("sides")(mine, near, off, *weights, acc)
    acc, high, low = after((acc, high, low))
    picked = jax.ShapeDtypeStruct((2 * LONG, PAIR), BF)
    to_near, to_off = vmem_call(pick_kernel, (picked, picked))(mine, near, off, high, low)
    far_near, far_off = swap(to_near, 1), swap(to_off, -1)
    acc = phase_call("middle")(mine, low, high, far_near, *weights, acc)
    velocity = phase_call("end")(mine, far_off, *weights, acc)
    return velocity.reshape(3, K, 1, 1, CELLS)


def solution(mesh):
    return jax.shard_map(
        local,
        mesh=mesh,
        in_specs=(
            P(None, None, "gx", "gy", None),
            P(),
            P(),
            P(),
            P("gx", "gy", None, None),
            P("gx", "gy", None, None),
            P("gx", "gy", None, None, None),
            P("gx", "gy", None),
        ),
        out_specs=P(None, None, "gx", "gy", None),
        check_vma=False,
    )
```

```python
import functools

import jax
import jax.numpy as jnp
from jax import lax
from jax.experimental import pallas as pl
from jax.experimental.pallas import tpu as pltpu
from jax.sharding import PartitionSpec as P

BF = jnp.bfloat16
F32 = jnp.float32

K = 289
MAIN = 256
REST = K - MAIN
TAIL = 128
WIDE = 3 * MAIN + TAIL
CELLS = 512
SLOTS = 128
NR = 16
CAP = 16
PAIR = 2 * SLOTS
GROUP = 2 * CAP
ROWS = NR * GROUP
LONG = 880
SLAB = 16
SLAB_AT = LONG - SLAB
HEAD = 13
ABOVE = SLAB - HEAD
BASE = 32
OWN, PARTNER = 0, 2
CODE = 9
ODD = 12
COLUMNS = (slice(0, 256), slice(256, 512), slice(512, 768), slice(768, 896))
VMEM_LIMIT = 28 * 1024 * 1024
HERE_COST = 30_000_000_000
PACK_LIMIT = 62 * 1024 * 1024


def nt(a, b):
    return lax.dot_general(a, b, (((1,), (1,)), ((), ())), preferred_element_type=F32)


def nn(a, b):
    return jnp.dot(a, b, preferred_element_type=F32)


def iota(shape, dim):
    return lax.broadcasted_iota(jnp.int32, shape, dim)


def where_one(condition):
    return jnp.where(condition, 1.0, 0.0).astype(BF)


def eye(size):
    return where_one(iota((size, size), 0) == iota((size, size), 1))


def spread(c):
    return where_one(iota((TAIL, REST), 0) == iota((TAIL, REST), 1) + c * REST)


def offset_of(dx, dy):
    return (dx + 1) * 3 + dy + 1


def offsets(side, dy):
    return offset_of(side, dy), offset_of(-side, dy)


def choose(even, side, dy, read, theirs=False):
    first, second = [8 - o if theirs else o for o in offsets(side, dy)]
    return read(first) if first == second else jnp.where(even, read(first), read(second))


def parity_lanes(width, start):
    k = iota((1, width), 1) + start
    degree = jnp.zeros((1, width), jnp.int32)
    for level in range(1, 17):
        degree = degree + jnp.where(k >= level * level, 1, 0)
    return 1.0 - 2.0 * (degree % 2).astype(F32)


def side_signs(width, start):
    signs = jnp.broadcast_to(parity_lanes(width, start), (GROUP, width))
    return jnp.where(iota((GROUP, width), 0) >= CAP, signs, 1.0)


def pick_table(own_side, partner_side):
    cells = iota((CELLS, SLOTS), 0)
    return jnp.concatenate([where_one(cells == own_side), where_one(cells == partner_side)], axis=1)


def ranks_of(rots):
    marks = [where_one(iota((NR, SLOTS), 0) == rot) for rot in rots]
    earlier = where_one(iota((SLOTS, SLOTS), 0) < iota((SLOTS, SLOTS), 1))
    counts = nn(jnp.concatenate(marks, axis=0), earlier)
    return [
        jnp.sum(mark.astype(F32) * counts[o * NR : (o + 1) * NR], axis=0, keepdims=True).astype(jnp.int32)
        for o, mark in enumerate(marks)
    ]


def place_rows(codes, lives):
    rows = [code + code // CAP * CAP + side * CAP for side, code in enumerate(codes)]
    return [jnp.where(live > 0.5, row, -1) for live, row in zip(lives, rows)]


def apply_dense(block, main_ref, tail_ref):
    tail = block[:, 3 * MAIN :]
    outs = [
        nt(jnp.concatenate([block[:, c * MAIN : (c + 1) * MAIN], tail], axis=1), main_ref[c]) for c in range(3)
    ]
    return outs + [nt(block, tail_ref[...])]


def split_lanes(block):
    return [block[:, c * MAIN : (c + 1) * MAIN] for c in range(3)], block[:, 3 * MAIN :]


def prep_kernel(rot_ref, trans_ref, self_ref, rot_tail, *pieces):
    fold = where_one((iota((TAIL, REST), 0) % REST == iota((TAIL, REST), 1)) & (iota((TAIL, REST), 0) < 3 * REST))
    same = (iota((TAIL, TAIL), 0) // REST) == (iota((TAIL, TAIL), 1) // REST)

    def tail_block(block):
        return jnp.where(same, nt(nn(fold, block).astype(BF), fold), 0.0).astype(BF)

    rot_tail[...] = jnp.zeros(rot_tail.shape, BF)
    for r in range(NR):
        place = slice(r % 2 * TAIL, (r % 2 + 1) * TAIL)
        rot_tail[r // 2, place, place] = tail_block(rot_ref[r, MAIN:, MAIN:])
    for source, (main, tail) in ((trans_ref, pieces[:2]), (self_ref, pieces[2:])):
        for c in range(3):
            main[c, :, :MAIN] = source[:MAIN, :MAIN]
            main[c, :, MAIN:] = nt(source[:MAIN, MAIN:], spread(c)).astype(BF)
            tail[:, c * MAIN : (c + 1) * MAIN] = nn(spread(c), source[MAIN:, :MAIN]).astype(BF)
        tail[:, 3 * MAIN :] = tail_block(source[MAIN:, MAIN:])


def head_part(ref, at, row, block):
    lanes = slice(block * SLOTS, (block + 1) * SLOTS)
    return ref[at : at + SLAB, lanes].astype(F32)[row + ABOVE : row + ABOVE + 1]


def head_cells(ref, what, row, at=SLAB_AT):
    return (head_part(ref, at, row, what) * BASE + head_part(ref, at, row, what + 1)).astype(jnp.int32)


def head_codes(ref, o):
    return head_part(ref, SLAB_AT, CODE + o // 4, o % 4).astype(jnp.int32)


def head_live(ref, o):
    lane = iota((1, SLOTS), 1)
    count = jnp.sum(jnp.where(lane == o, head_part(ref, SLAB_AT, ODD, 1), 0.0), axis=1, keepdims=True)
    return jnp.where(lane.astype(F32) < count, 1.0, 0.0)


def is_even(mine):
    return head_part(mine, SLAB_AT, ODD, 0) < 0.5


def head_digits(index):
    high = index // BASE
    return high.astype(F32).astype(BF), (index - high * BASE).astype(F32).astype(BF)


def pack_kernel(count_ref, own_ref, partner_ref, rot_ref, here_ref, out, *scratch):
    held, tail, arrived, sent = scratch[:5], scratch[5], scratch[6], scratch[7]
    count, own, partner, rot, here = held
    small = [
        pltpu.make_async_copy(src, dst, arrived.at[3 + i])
        for i, (src, dst) in enumerate(zip((count_ref, own_ref, partner_ref, rot_ref), held))
    ]
    bodies = [pltpu.make_async_copy(here_ref.at[c], here.at[c], arrived.at[c]) for c in range(3)]
    for copy in small + bodies:
        copy.start()
    for copy in small:
        copy.wait()
    slot = iota((1, SLOTS), 1)
    ranks = ranks_of([rot[o] for o in range(9)])
    codes = [(rot[o] * CAP + ranks[o]).astype(F32) for o in range(9)]
    codes.extend([jnp.zeros((1, SLOTS), F32)] * 3)
    code_rows = [jnp.concatenate(codes[4 * i : 4 * i + 4], axis=1) for i in range(3)]
    cells = [jnp.concatenate([ref[o] for o in range(9)], axis=0) for ref in (own, partner)]
    digits = jnp.concatenate([d.astype(F32) for index in cells for d in head_digits(index)], axis=1)
    odd = lax.rem(lax.axis_index("gx"), 2)
    counts = jnp.zeros((1, SLOTS), jnp.int32)
    for o in range(9):
        counts = jnp.where(slot == o, count[0, o], counts)
    flags = [jnp.where(slot * 0 + odd > 0, 1.0, 0.0), counts.astype(F32), jnp.zeros((1, 2 * SLOTS), F32)]
    head = jnp.concatenate([jnp.zeros((3 * REST, CELLS), F32), digits, *code_rows, jnp.concatenate(flags, axis=1)], axis=0)
    sends = [
        pltpu.make_async_copy(here.at[c, :MAIN], out.at[c * MAIN : (c + 1) * MAIN], sent.at[c]) for c in range(3)
    ]
    for body, send in zip(bodies, sends):
        body.wait()
        send.start()
    rest = nn(spread(0), here[0, MAIN:]) + nn(spread(1), here[1, MAIN:]) + nn(spread(2), here[2, MAIN:])
    tail[...] = (rest[: LONG - 3 * MAIN] + head).astype(BF)
    last = pltpu.make_async_copy(tail, out.at[3 * MAIN :], sent.at[3])
    last.start()
    for copy in sends + [last]:
        copy.wait()


def pick_kernel(mine, near, off, high, low, to_near, to_off):
    even = is_even(mine)
    for i, (source, dy) in enumerate(((low, -1), (high, 1))):
        for side, target, out in ((-1, near, to_near), (1, off, to_off)):
            wanted = choose(even, side, dy, lambda o: head_cells(target, PARTNER, o))
            owners = choose(even, side, dy, lambda o: head_cells(source, OWN, o), True)
            picked = nn(source[...], pick_table(wanted, owners))
            out[i * LONG : i * LONG + SLAB_AT] = picked[:SLAB_AT].astype(BF)
            digits = head_digits(choose(even, side, dy, lambda o: head_cells(source, PARTNER, o), True))
            cells = jnp.concatenate([d.astype(F32) for d in digits], axis=1)
            code = choose(even, side, dy, lambda o: head_codes(source, o), True).astype(F32)
            live = choose(even, side, dy, lambda o: head_live(source, o), True)
            row = iota((SLAB, PAIR), 0) - ABOVE
            head = jnp.zeros((SLAB, PAIR), F32)
            for number, line in enumerate((cells, jnp.concatenate([code, code], axis=1), jnp.concatenate([live, live], axis=1))):
                head = jnp.where(row == number, line, head)
            slab = jnp.where(row < 0, picked[SLAB_AT:], head)
            out[i * LONG + SLAB_AT : (i + 1) * LONG] = slab.astype(BF)


PHASES = {
    "here": ((0, 0),),
    "sides": ((1, 0), (-1, 0)),
    "middle": ((0, -1), (0, 1), (1, -1), (1, 1)),
    "end": ((-1, -1), (-1, 1)),
}


def phase_kernel(kind, *refs):
    sources = PHASES[kind]
    first, last = kind == "here", kind == "end"
    m = len(sources)
    mine = refs[0]
    even = is_even(mine)
    count = {"here": 1, "sides": 3, "middle": 4, "end": 2}[kind]
    arrays, refs = refs[:count], refs[count:]
    rot_ref, rot_tail, trans_main, trans_tail = refs[:4]
    refs = refs[4:]
    if first:
        self_main, self_tail = refs[:2]
        refs = refs[2:]
    else:
        acc_in = refs[0]
        refs = refs[1:]
    out, grouped, turned, places_to = refs

    def forwarded(s):
        side, dy = sources[s]
        return side and dy

    def other(s):
        side, dy = sources[s]
        if forwarded(s):
            return arrays[-1], (0 if dy < 0 else LONG)
        return arrays[s if first else s + 1], 0

    def cell_pair(s, mine_what, their_what):
        array, start = other(s)
        ours = choose(even, *sources[s], lambda o: head_cells(mine, mine_what, o))
        if forwarded(s):
            return ours, head_cells(array, OWN, 0, start + SLAB_AT)
        return ours, choose(even, *sources[s], lambda o: head_cells(array, their_what, o), True)

    def place_pair(s):
        array, start = other(s)
        codes = [choose(even, *sources[s], lambda o: head_codes(mine, o))]
        lives = [choose(even, *sources[s], lambda o: head_live(mine, o))]
        if forwarded(s):
            codes.append(head_part(array, start + SLAB_AT, 1, 0).astype(jnp.int32))
            lives.append(head_part(array, start + SLAB_AT, 2, 0))
        else:
            codes.append(choose(even, *sources[s], lambda o: head_codes(array, o), True))
            lives.append(choose(even, *sources[s], lambda o: head_live(array, o), True))
        return place_rows(codes, lives)

    if first:
        whole = jnp.concatenate([mine[...], jnp.zeros((WIDE - LONG, CELLS), BF)], axis=0)
        rows = nt(eye(CELLS), whole).astype(BF)
        for lanes, part in zip(COLUMNS, apply_dense(rows, self_main, self_tail)):
            out[:, lanes] = part

    for s in range(m):
        array, start = other(s)
        if forwarded(s):
            taken = array[start : start + LONG]
        else:
            table = pick_table(*cell_pair(s, PARTNER, OWN))
            taken = nn(array[...], table).astype(BF)
        row_ids = iota((ROWS, SLOTS), 0)
        own_place, partner_place = place_pair(s)
        place = jnp.concatenate([where_one(row_ids == own_place), where_one(row_ids == partner_place)], axis=1)
        lanes = slice(s * GROUP, (s + 1) * GROUP)
        taken = jnp.concatenate([taken, jnp.zeros((WIDE - LONG, PAIR), BF)], axis=0)
        grouped[:, lanes, :] = nt(place, taken).astype(BF).reshape(NR, GROUP, WIDE)
        own_to, partner_to = cell_pair(s, OWN, PARTNER)
        to = jnp.concatenate([own_to, partner_to], axis=1) + 1
        digits = jnp.concatenate([to // BASE, to % BASE, jnp.zeros((6, PAIR), jnp.int32)], axis=0)
        back = nt(digits.astype(F32).astype(BF), place)
        goal = (back[0:1] * BASE + back[1:2]).astype(jnp.int32) - 1
        places_to[:, s * ROWS : (s + 1) * ROWS] = where_one(iota((CELLS, ROWS), 0) == goal)

    size = m * GROUP
    main_signs = side_signs(MAIN, 0)

    def turn(pair, source, target, dot):
        tails = []
        for r in (2 * pair, 2 * pair + 1):
            mains, tail = split_lanes(source[r])
            tails.append(tail)
            turned_main = dot(jnp.concatenate(mains, axis=0), rot_ref[r, :MAIN, :MAIN])
            turned_main = (turned_main.reshape(3 * m, GROUP, MAIN) * main_signs[None]).reshape(3 * size, MAIN)
            for c in range(3):
                target[r, :, c * MAIN : (c + 1) * MAIN] = turned_main[c * size : (c + 1) * size].astype(BF)
        both = dot(jnp.concatenate(tails, axis=1), rot_tail[pair]).astype(BF)
        target[2 * pair, :, 3 * MAIN :] = both[:, :TAIL]
        target[2 * pair + 1, :, 3 * MAIN :] = both[:, TAIL:]

    for pair in range(NR // 2):
        turn(pair, grouped, turned, nt)

    block = turned[...].reshape(NR * size, WIDE)
    for lanes, part in zip(COLUMNS, apply_dense(block, trans_main, trans_tail)):
        grouped[:, :, lanes] = part.astype(BF).reshape(NR, size, lanes.stop - lanes.start)

    for pair in range(NR // 2):
        turn(pair, grouped, turned, nn)

    for c, lanes in enumerate(COLUMNS):
        width = lanes.stop - lanes.start
        back = [turned[:, s * GROUP : (s + 1) * GROUP, lanes].reshape(ROWS, width) for s in range(m)]
        total = nn(places_to[...], jnp.concatenate(back, axis=0))
        total = total + (out[:, lanes] if first else acc_in[:, lanes])
        if not last:
            out[:, lanes] = total
        elif c < 3:
            out[c, :MAIN, :] = total.astype(BF).T
        else:
            tail = total.astype(BF).T
            for part in range(3):
                gather = where_one(iota((REST, TAIL), 1) == iota((REST, TAIL), 0) + part * REST)
                out[part, MAIN:, :] = nn(gather, tail).astype(BF)


def vmem_call(kernel, out_shape, scratch=(), limit=VMEM_LIMIT, cost=1000, **options):
    return pl.pallas_call(
        kernel,
        out_shape=out_shape,
        scratch_shapes=list(scratch),
        compiler_params=pltpu.CompilerParams(vmem_limit_bytes=limit),
        cost_estimate=pl.CostEstimate(flops=cost, bytes_accessed=1000, transcendentals=0),
        **options,
    )


def phase_call(kind):
    m, last = len(PHASES[kind]), kind == "end"
    if last:
        out = jax.ShapeDtypeStruct((3, K, CELLS), BF)
    else:
        out = jax.ShapeDtypeStruct((CELLS, WIDE), F32)
    scratch = [
        pltpu.VMEM((NR, m * GROUP, WIDE), BF),
        pltpu.VMEM((NR, m * GROUP, WIDE), BF),
        pltpu.VMEM((CELLS, m * ROWS), BF),
    ]
    cost = HERE_COST if kind == "here" else 1000
    return vmem_call(functools.partial(phase_kernel, kind), out, scratch, cost=cost)


def swap(block, first):
    count = lax.axis_size("gx")
    return lax.ppermute(block, "gx", [(i, (i + (first if i % 2 == 0 else -first)) % count) for i in range(count)])


def shift(block, axis, distance):
    count = lax.axis_size(axis)
    return lax.ppermute(block, axis, [((i - distance) % count, i) for i in range(count)])


def local(traction, self_operator, translation, rotations, own_cell, partner_cell, rot_index, block_count):
    here = traction.reshape(3, K, CELLS)
    slots = [a.reshape(9, 1, SLOTS) for a in (own_cell, partner_cell, rot_index)]
    there = pl.BlockSpec(memory_space=pl.ANY)
    mine = vmem_call(
        pack_kernel,
        jax.ShapeDtypeStruct((LONG, CELLS), BF),
        [pltpu.SMEM((1, 9), jnp.int32)]
        + [pltpu.VMEM((9, 1, SLOTS), jnp.int32)] * 3
        + [pltpu.VMEM((3, K, CELLS), BF), pltpu.VMEM((LONG - 3 * MAIN, CELLS), BF)]
        + [pltpu.SemaphoreType.DMA((7,)), pltpu.SemaphoreType.DMA((4,))],
        limit=PACK_LIMIT,
        in_specs=[there] * 5,
        out_specs=there,
    )(block_count.reshape(1, 9), *slots, here)
    after = lax.optimization_barrier
    near, off = swap(mine, 1), swap(mine, -1)
    high, low = shift(mine, "gy", -1), shift(mine, "gy", 1)

    dense = [
        jax.ShapeDtypeStruct((3, MAIN, MAIN + TAIL), BF),
        jax.ShapeDtypeStruct((TAIL, WIDE), BF),
    ]
    rot_tail, *dense = vmem_call(
        prep_kernel, [jax.ShapeDtypeStruct((NR // 2, 2 * TAIL, 2 * TAIL), BF)] + dense + dense
    )(rotations, translation, self_operator)
    weights = (rotations, rot_tail, *dense[:2])

    acc = phase_call("here")(mine, *weights, *dense[2:])
    acc = phase_call("sides")(mine, near, off, *weights, acc)
    acc, high, low = after((acc, high, low))
    picked = jax.ShapeDtypeStruct((2 * LONG, PAIR), BF)
    to_near, to_off = vmem_call(pick_kernel, (picked, picked))(mine, near, off, high, low)
    far_near, far_off = swap(to_near, 1), swap(to_off, -1)
    acc = phase_call("middle")(mine, low, high, far_near, *weights, acc)
    velocity = phase_call("end")(mine, far_off, *weights, acc)
    return velocity.reshape(3, K, 1, 1, CELLS)


def solution(mesh):
    return jax.shard_map(
        local,
        mesh=mesh,
        in_specs=(
            P(None, None, "gx", "gy", None),
            P(),
            P(),
            P(),
            P("gx", "gy", None, None),
            P("gx", "gy", None, None),
            P("gx", "gy", None, None, None),
            P("gx", "gy", None),
        ),
        out_specs=P(None, None, "gx", "gy", None),
        check_vma=False,
    )
```

```python
import functools

import jax
import jax.numpy as jnp
from jax import lax
from jax.experimental import pallas as pl
from jax.experimental.pallas import tpu as pltpu
from jax.sharding import PartitionSpec as P

BF = jnp.bfloat16
F32 = jnp.float32

K = 289
MAIN = 256
REST = K - MAIN
TAIL = 128
WIDE = 3 * MAIN + TAIL
CELLS = 512
SLOTS = 128
NR = 16
CAP = 16
PAIR = 2 * SLOTS
GROUP = 2 * CAP
ROWS = NR * GROUP
LONG = 880
SLAB = 16
SLAB_AT = LONG - SLAB
HEAD = 13
ABOVE = SLAB - HEAD
BASE = 32
OWN, PARTNER = 0, 2
CODE = 9
ODD = 12
COLUMNS = (slice(0, 256), slice(256, 512), slice(512, 768), slice(768, 896))
VMEM_LIMIT = 28 * 1024 * 1024
HERE_COST = 30_000_000_000
PACK_LIMIT = 62 * 1024 * 1024


def nt(a, b):
    return lax.dot_general(a, b, (((1,), (1,)), ((), ())), preferred_element_type=F32)


def nn(a, b):
    return jnp.dot(a, b, preferred_element_type=F32)


def iota(shape, dim):
    return lax.broadcasted_iota(jnp.int32, shape, dim)


def where_one(condition):
    return jnp.where(condition, 1.0, 0.0).astype(BF)


def eye(size):
    return where_one(iota((size, size), 0) == iota((size, size), 1))


def spread(c):
    return where_one(iota((TAIL, REST), 0) == iota((TAIL, REST), 1) + c * REST)


def offset_of(dx, dy):
    return (dx + 1) * 3 + dy + 1


def offsets(side, dy):
    return offset_of(side, dy), offset_of(-side, dy)


def choose(even, side, dy, read, theirs=False):
    first, second = [8 - o if theirs else o for o in offsets(side, dy)]
    return read(first) if first == second else jnp.where(even, read(first), read(second))


def parity_lanes(width, start):
    k = iota((1, width), 1) + start
    degree = jnp.zeros((1, width), jnp.int32)
    for level in range(1, 17):
        degree = degree + jnp.where(k >= level * level, 1, 0)
    return 1.0 - 2.0 * (degree % 2).astype(F32)


def side_signs(width, start):
    signs = jnp.broadcast_to(parity_lanes(width, start), (GROUP, width))
    return jnp.where(iota((GROUP, width), 0) >= CAP, signs, 1.0)


def pick_table(own_side, partner_side):
    cells = iota((CELLS, SLOTS), 0)
    return jnp.concatenate([where_one(cells == own_side), where_one(cells == partner_side)], axis=1)


def ranks_of(rots):
    marks = [where_one(iota((NR, SLOTS), 0) == rot) for rot in rots]
    earlier = where_one(iota((SLOTS, SLOTS), 0) < iota((SLOTS, SLOTS), 1))
    counts = nn(jnp.concatenate(marks, axis=0), earlier)
    return [
        jnp.sum(mark.astype(F32) * counts[o * NR : (o + 1) * NR], axis=0, keepdims=True).astype(jnp.int32)
        for o, mark in enumerate(marks)
    ]


def place_rows(codes, lives):
    rows = [code + code // CAP * CAP + side * CAP for side, code in enumerate(codes)]
    return [jnp.where(live, row, -1) for live, row in zip(lives, rows)]


def apply_dense(block, main_ref, tail_ref):
    tail = block[:, 3 * MAIN :]
    outs = [
        nt(jnp.concatenate([block[:, c * MAIN : (c + 1) * MAIN], tail], axis=1), main_ref[c]) for c in range(3)
    ]
    return outs + [nt(block, tail_ref[...])]


def split_lanes(block):
    return [block[:, c * MAIN : (c + 1) * MAIN] for c in range(3)], block[:, 3 * MAIN :]


def prep_kernel(rot_ref, trans_ref, self_ref, rot_tail, *pieces):
    fold = where_one((iota((TAIL, REST), 0) % REST == iota((TAIL, REST), 1)) & (iota((TAIL, REST), 0) < 3 * REST))
    same = (iota((TAIL, TAIL), 0) // REST) == (iota((TAIL, TAIL), 1) // REST)

    def tail_block(block):
        return jnp.where(same, nt(nn(fold, block).astype(BF), fold), 0.0).astype(BF)

    rot_tail[...] = jnp.zeros(rot_tail.shape, BF)
    for r in range(NR):
        place = slice(r % 2 * TAIL, (r % 2 + 1) * TAIL)
        rot_tail[r // 2, place, place] = tail_block(rot_ref[r, MAIN:, MAIN:])
    for source, (main, tail) in ((trans_ref, pieces[:2]), (self_ref, pieces[2:])):
        for c in range(3):
            main[c, :, :MAIN] = source[:MAIN, :MAIN]
            main[c, :, MAIN:] = nt(source[:MAIN, MAIN:], spread(c)).astype(BF)
            tail[:, c * MAIN : (c + 1) * MAIN] = nn(spread(c), source[MAIN:, :MAIN]).astype(BF)
        tail[:, 3 * MAIN :] = tail_block(source[MAIN:, MAIN:])


def head_part(ref, at, row, block):
    lanes = slice(block * SLOTS, (block + 1) * SLOTS)
    return ref[at : at + SLAB, lanes].astype(F32)[row + ABOVE : row + ABOVE + 1]


def head_cells(ref, what, row, at=SLAB_AT):
    return (head_part(ref, at, row, what) * BASE + head_part(ref, at, row, what + 1)).astype(jnp.int32)


def head_codes(ref, o):
    return head_part(ref, SLAB_AT, CODE + o // 4, o % 4).astype(jnp.int32)


def live_slots(even, side, dy, counts, theirs=False):
    lane = iota((1, SLOTS), 1)
    block = choose(even, side, dy, lambda o: o, theirs)
    count = jnp.sum(jnp.where(lane == block, counts, 0.0), axis=1, keepdims=True)
    return lane.astype(F32) < count


def is_even(mine):
    return head_part(mine, SLAB_AT, ODD, 0) < 0.5


def head_digits(index):
    high = index // BASE
    return high.astype(F32).astype(BF), (index - high * BASE).astype(F32).astype(BF)


def pack_kernel(count_ref, own_ref, partner_ref, rot_ref, here_ref, out, *scratch):
    held, tail, arrived, sent = scratch[:5], scratch[5], scratch[6], scratch[7]
    count, own, partner, rot, here = held
    small = [
        pltpu.make_async_copy(src, dst, arrived.at[3 + i])
        for i, (src, dst) in enumerate(zip((count_ref, own_ref, partner_ref, rot_ref), held))
    ]
    bodies = [pltpu.make_async_copy(here_ref.at[c], here.at[c], arrived.at[c]) for c in range(3)]
    for copy in small + bodies:
        copy.start()
    for copy in small:
        copy.wait()
    slot = iota((1, SLOTS), 1)
    ranks = ranks_of([rot[o] for o in range(9)])
    codes = [(rot[o] * CAP + ranks[o]).astype(F32) for o in range(9)]
    codes.extend([jnp.zeros((1, SLOTS), F32)] * 3)
    code_rows = [jnp.concatenate(codes[4 * i : 4 * i + 4], axis=1) for i in range(3)]
    cells = [jnp.concatenate([ref[o] for o in range(9)], axis=0) for ref in (own, partner)]
    digits = jnp.concatenate([d.astype(F32) for index in cells for d in head_digits(index)], axis=1)
    odd = lax.rem(lax.axis_index("gx"), 2)
    counts = jnp.zeros((1, SLOTS), jnp.int32)
    for o in range(9):
        counts = jnp.where(slot == o, count[0, o], counts)
    flags = [jnp.where(slot * 0 + odd > 0, 1.0, 0.0), counts.astype(F32), jnp.zeros((1, 2 * SLOTS), F32)]
    head = jnp.concatenate([jnp.zeros((3 * REST, CELLS), F32), digits, *code_rows, jnp.concatenate(flags, axis=1)], axis=0)
    sends = [
        pltpu.make_async_copy(here.at[c, :MAIN], out.at[c * MAIN : (c + 1) * MAIN], sent.at[c]) for c in range(3)
    ]
    for body, send in zip(bodies, sends):
        body.wait()
        send.start()
    rest = nn(spread(0), here[0, MAIN:]) + nn(spread(1), here[1, MAIN:]) + nn(spread(2), here[2, MAIN:])
    tail[...] = (rest[: LONG - 3 * MAIN] + head).astype(BF)
    last = pltpu.make_async_copy(tail, out.at[3 * MAIN :], sent.at[3])
    last.start()
    for copy in sends + [last]:
        copy.wait()


def pick_kernel(mine, near, off, high, low, to_near, to_off):
    even = is_even(mine)
    for i, (source, dy) in enumerate(((low, -1), (high, 1))):
        for side, target, out in ((-1, near, to_near), (1, off, to_off)):
            wanted = choose(even, side, dy, lambda o: head_cells(target, PARTNER, o))
            owners = choose(even, side, dy, lambda o: head_cells(source, OWN, o), True)
            picked = nn(source[...], pick_table(wanted, owners))
            out[i * LONG : i * LONG + SLAB_AT] = picked[:SLAB_AT].astype(BF)
            digits = head_digits(choose(even, side, dy, lambda o: head_cells(source, PARTNER, o), True))
            cells = jnp.concatenate([d.astype(F32) for d in digits], axis=1)
            code = choose(even, side, dy, lambda o: head_codes(source, o), True).astype(F32)
            counts = head_part(source, SLAB_AT, ODD, 1)
            row = iota((SLAB, PAIR), 0) - ABOVE
            head = jnp.zeros((SLAB, PAIR), F32)
            doubled = [jnp.concatenate([line, line], axis=1) for line in (code, counts)]
            for number, line in enumerate((cells, *doubled)):
                head = jnp.where(row == number, line, head)
            slab = jnp.where(row < 0, picked[SLAB_AT:], head)
            out[i * LONG + SLAB_AT : (i + 1) * LONG] = slab.astype(BF)


PHASES = {
    "here": ((0, 0),),
    "sides": ((1, 0), (-1, 0)),
    "middle": ((0, -1), (0, 1), (1, -1), (1, 1)),
    "end": ((-1, -1), (-1, 1)),
}


def phase_kernel(kind, *refs):
    sources = PHASES[kind]
    first, last = kind == "here", kind == "end"
    m = len(sources)
    mine = refs[0]
    even = is_even(mine)
    count = {"here": 1, "sides": 3, "middle": 4, "end": 2}[kind]
    arrays, refs = refs[:count], refs[count:]
    rot_ref, rot_tail, trans_main, trans_tail = refs[:4]
    refs = refs[4:]
    if first:
        self_main, self_tail = refs[:2]
        refs = refs[2:]
    else:
        acc_in = refs[0]
        refs = refs[1:]
    out, grouped, turned, places_to = refs

    def forwarded(s):
        side, dy = sources[s]
        return side and dy

    def other(s):
        side, dy = sources[s]
        if forwarded(s):
            return arrays[-1], (0 if dy < 0 else LONG)
        return arrays[s if first else s + 1], 0

    def cell_pair(s, mine_what, their_what):
        array, start = other(s)
        ours = choose(even, *sources[s], lambda o: head_cells(mine, mine_what, o))
        if forwarded(s):
            return ours, head_cells(array, OWN, 0, start + SLAB_AT)
        return ours, choose(even, *sources[s], lambda o: head_cells(array, their_what, o), True)

    def place_pair(s):
        array, start = other(s)
        codes = [choose(even, *sources[s], lambda o: head_codes(mine, o))]
        if forwarded(s):
            codes.append(head_part(array, start + SLAB_AT, 1, 0).astype(jnp.int32))
            counts = head_part(array, start + SLAB_AT, 2, 0)
        else:
            codes.append(choose(even, *sources[s], lambda o: head_codes(array, o), True))
            counts = head_part(array, SLAB_AT, ODD, 1)
        lives = [
            live_slots(even, *sources[s], head_part(mine, SLAB_AT, ODD, 1)),
            live_slots(even, *sources[s], counts, True),
        ]
        return place_rows(codes, lives)

    if first:
        whole = jnp.concatenate([mine[...], jnp.zeros((WIDE - LONG, CELLS), BF)], axis=0)
        rows = nt(eye(CELLS), whole).astype(BF)
        for lanes, part in zip(COLUMNS, apply_dense(rows, self_main, self_tail)):
            out[:, lanes] = part

    for s in range(m):
        array, start = other(s)
        if forwarded(s):
            taken = array[start : start + LONG]
        else:
            table = pick_table(*cell_pair(s, PARTNER, OWN))
            taken = nn(array[...], table).astype(BF)
        row_ids = iota((ROWS, SLOTS), 0)
        own_place, partner_place = place_pair(s)
        place = jnp.concatenate([where_one(row_ids == own_place), where_one(row_ids == partner_place)], axis=1)
        lanes = slice(s * GROUP, (s + 1) * GROUP)
        taken = jnp.concatenate([taken, jnp.zeros((WIDE - LONG, PAIR), BF)], axis=0)
        grouped[:, lanes, :] = nt(place, taken).astype(BF).reshape(NR, GROUP, WIDE)
        own_to, partner_to = cell_pair(s, OWN, PARTNER)
        to = jnp.concatenate([own_to, partner_to], axis=1) + 1
        digits = jnp.concatenate([to // BASE, to % BASE, jnp.zeros((6, PAIR), jnp.int32)], axis=0)
        back = nt(digits.astype(F32).astype(BF), place)
        goal = (back[0:1] * BASE + back[1:2]).astype(jnp.int32) - 1
        places_to[:, s * ROWS : (s + 1) * ROWS] = where_one(iota((CELLS, ROWS), 0) == goal)

    size = m * GROUP
    main_signs = side_signs(MAIN, 0)

    def turn(pair, source, target, dot):
        tails = []
        for r in (2 * pair, 2 * pair + 1):
            mains, tail = split_lanes(source[r])
            tails.append(tail)
            turned_main = dot(jnp.concatenate(mains, axis=0), rot_ref[r, :MAIN, :MAIN])
            turned_main = (turned_main.reshape(3 * m, GROUP, MAIN) * main_signs[None]).reshape(3 * size, MAIN)
            for c in range(3):
                target[r, :, c * MAIN : (c + 1) * MAIN] = turned_main[c * size : (c + 1) * size].astype(BF)
        both = dot(jnp.concatenate(tails, axis=1), rot_tail[pair]).astype(BF)
        target[2 * pair, :, 3 * MAIN :] = both[:, :TAIL]
        target[2 * pair + 1, :, 3 * MAIN :] = both[:, TAIL:]

    for pair in range(NR // 2):
        turn(pair, grouped, turned, nt)

    block = turned[...].reshape(NR * size, WIDE)
    for lanes, part in zip(COLUMNS, apply_dense(block, trans_main, trans_tail)):
        grouped[:, :, lanes] = part.astype(BF).reshape(NR, size, lanes.stop - lanes.start)

    for pair in range(NR // 2):
        turn(pair, grouped, turned, nn)

    for c, lanes in enumerate(COLUMNS):
        width = lanes.stop - lanes.start
        back = [turned[:, s * GROUP : (s + 1) * GROUP, lanes].reshape(ROWS, width) for s in range(m)]
        total = nn(places_to[...], jnp.concatenate(back, axis=0))
        total = total + (out[:, lanes] if first else acc_in[:, lanes])
        if not last:
            out[:, lanes] = total
        elif c < 3:
            out[c, :MAIN, :] = total.astype(BF).T
        else:
            tail = total.astype(BF).T
            for part in range(3):
                gather = where_one(iota((REST, TAIL), 1) == iota((REST, TAIL), 0) + part * REST)
                out[part, MAIN:, :] = nn(gather, tail).astype(BF)


def vmem_call(kernel, out_shape, scratch=(), limit=VMEM_LIMIT, cost=1000, **options):
    return pl.pallas_call(
        kernel,
        out_shape=out_shape,
        scratch_shapes=list(scratch),
        compiler_params=pltpu.CompilerParams(vmem_limit_bytes=limit),
        cost_estimate=pl.CostEstimate(flops=cost, bytes_accessed=1000, transcendentals=0),
        **options,
    )


def phase_call(kind):
    m, last = len(PHASES[kind]), kind == "end"
    if last:
        out = jax.ShapeDtypeStruct((3, K, CELLS), BF)
    else:
        out = jax.ShapeDtypeStruct((CELLS, WIDE), F32)
    scratch = [
        pltpu.VMEM((NR, m * GROUP, WIDE), BF),
        pltpu.VMEM((NR, m * GROUP, WIDE), BF),
        pltpu.VMEM((CELLS, m * ROWS), BF),
    ]
    cost = HERE_COST if kind == "here" else 1000
    return vmem_call(functools.partial(phase_kernel, kind), out, scratch, cost=cost)


def swap(block, first):
    count = lax.axis_size("gx")
    return lax.ppermute(block, "gx", [(i, (i + (first if i % 2 == 0 else -first)) % count) for i in range(count)])


def shift(block, axis, distance):
    count = lax.axis_size(axis)
    return lax.ppermute(block, axis, [((i - distance) % count, i) for i in range(count)])


def local(traction, self_operator, translation, rotations, own_cell, partner_cell, rot_index, block_count):
    here = traction.reshape(3, K, CELLS)
    slots = [a.reshape(9, 1, SLOTS) for a in (own_cell, partner_cell, rot_index)]
    there = pl.BlockSpec(memory_space=pl.ANY)
    mine = vmem_call(
        pack_kernel,
        jax.ShapeDtypeStruct((LONG, CELLS), BF),
        [pltpu.SMEM((1, 9), jnp.int32)]
        + [pltpu.VMEM((9, 1, SLOTS), jnp.int32)] * 3
        + [pltpu.VMEM((3, K, CELLS), BF), pltpu.VMEM((LONG - 3 * MAIN, CELLS), BF)]
        + [pltpu.SemaphoreType.DMA((7,)), pltpu.SemaphoreType.DMA((4,))],
        limit=PACK_LIMIT,
        in_specs=[there] * 5,
        out_specs=there,
    )(block_count.reshape(1, 9), *slots, here)
    after = lax.optimization_barrier
    near, off = swap(mine, 1), swap(mine, -1)
    high, low = shift(mine, "gy", -1), shift(mine, "gy", 1)

    dense = [
        jax.ShapeDtypeStruct((3, MAIN, MAIN + TAIL), BF),
        jax.ShapeDtypeStruct((TAIL, WIDE), BF),
    ]
    rot_tail, *dense = vmem_call(
        prep_kernel, [jax.ShapeDtypeStruct((NR // 2, 2 * TAIL, 2 * TAIL), BF)] + dense + dense
    )(rotations, translation, self_operator)
    weights = (rotations, rot_tail, *dense[:2])

    acc = phase_call("here")(mine, *weights, *dense[2:])
    acc = phase_call("sides")(mine, near, off, *weights, acc)
    acc, high, low = after((acc, high, low))
    picked = jax.ShapeDtypeStruct((2 * LONG, PAIR), BF)
    to_near, to_off = vmem_call(pick_kernel, (picked, picked))(mine, near, off, high, low)
    far_near, far_off = swap(to_near, 1), swap(to_off, -1)
    acc = phase_call("middle")(mine, low, high, far_near, *weights, acc)
    velocity = phase_call("end")(mine, far_off, *weights, acc)
    return velocity.reshape(3, K, 1, 1, CELLS)


def solution(mesh):
    return jax.shard_map(
        local,
        mesh=mesh,
        in_specs=(
            P(None, None, "gx", "gy", None),
            P(),
            P(),
            P(),
            P("gx", "gy", None, None),
            P("gx", "gy", None, None),
            P("gx", "gy", None, None, None),
            P("gx", "gy", None),
        ),
        out_specs=P(None, None, "gx", "gy", None),
        check_vma=False,
    )
```
